128 devices in a mesh: dp: 32 (over z, y_lo, x), mp: 4 (over y_hi, core).
Axes of the slice: x: 4, y: 4 (y_hi: 2, y_lo: 2; y = y_hi * 2 + y_lo), z: 4, core: 2. Of those that a mesh axis runs over, the one named last changes fastest.
Arguments:
- tokens: bfloat16 [16384, 1024], P(('dp', 'mp')), may hold values from -6 to 6
- cotangent: bfloat16 [16384, 1024], P(('dp', 'mp')), may hold values from -6 to 6
- image_ids: int32 [32, 512], P('dp'), may hold values from 0 to 1, as said below
- valid_counts: int32 [32], P('dp'), may hold values from 448 to 512, as said below
- attend_weight: float32 [2, 1024, 3, 1024], P(None, 'dp', None, 'mp'), may hold values from -0.1875 to 0.1875
- output_weight: float32 [2, 1024, 1024], P(None, 'mp', 'dp'), may hold values from -0.75 to 0.75
- expand_weight: float32 [2, 1024, 4096], P(None, 'dp', 'mp'), may hold values from -0.1875 to 0.1875
- reduce_weight: float32 [2, 4096, 1024], P(None, 'mp', 'dp'), may hold values from -0.09375 to 0.09375
- vector_params: float32 [2, 14, 1024], P(None, None, 'dp'), may hold values from -2 to 2, as said below
- attend_first: float32 [2, 1024, 3, 1024], P(None, 'dp', None, 'mp'), may hold values from -40 to 40
- output_first: float32 [2, 1024, 1024], P(None, 'mp', 'dp'), may hold values from -20 to 20
- expand_first: float32 [2, 1024, 4096], P(None, 'dp', 'mp'), may hold values from -24 to 24
- reduce_first: float32 [2, 4096, 1024], P(None, 'mp', 'dp'), may hold values from -56 to 56
- vector_first: float32 [2, 14, 1024], P(None, None, 'dp'), may hold values from -48 to 48
- attend_second: float32 [2, 1024, 3, 1024], P(None, 'dp', None, 'mp'), may hold values from 4.096 to 16.384
- output_second: float32 [2, 1024, 1024], P(None, 'mp', 'dp'), may hold values from 1.024 to 4.096
- expand_second: float32 [2, 1024, 4096], P(None, 'dp', 'mp'), may hold values from 1.47456 to 5.89824
- reduce_second: float32 [2, 4096, 1024], P(None, 'mp', 'dp'), may hold values from 6.88128 to 27.8528
- vector_second: float32 [2, 14, 1024], P(None, None, 'dp'), may hold values from 65.536 to 262.144
Outputs:
- block_out: float32 [16384, 1024], P(('dp', 'mp'))
- tokens_grad: float32 [16384, 1024], P(('dp', 'mp'))
- attend_new: float32 [2, 1024, 3, 1024], P(None, 'dp', None, 'mp')
- output_new: float32 [2, 1024, 1024], P(None, 'mp', 'dp')
- expand_new: float32 [2, 1024, 4096], P(None, 'dp', 'mp')
- reduce_new: float32 [2, 4096, 1024], P(None, 'mp', 'dp')
- vector_new: float32 [2, 14, 1024], P(None, None, 'dp')
- attend_moment: float32 [2, 1024, 3, 1024], P(None, 'dp', None, 'mp')
- output_moment: float32 [2, 1024, 1024], P(None, 'mp', 'dp')
- expand_moment: float32 [2, 1024, 4096], P(None, 'dp', 'mp')
- reduce_moment: float32 [2, 4096, 1024], P(None, 'mp', 'dp')
- vector_moment: float32 [2, 14, 1024], P(None, None, 'dp')
- attend_square: float32 [2, 1024, 3, 1024], P(None, 'dp', None, 'mp')
- output_square: float32 [2, 1024, 1024], P(None, 'mp', 'dp')
- expand_square: float32 [2, 1024, 4096], P(None, 'dp', 'mp')
- reduce_square: float32 [2, 4096, 1024], P(None, 'mp', 'dp')
- vector_square: float32 [2, 14, 1024], P(None, None, 'dp')
The draws below stay inside these ranges and needn't reach their ends.
Inputs may be any that keep to these rules, and one draw needn't show every extreme that they name: `image_ids`: in each replica the ids never fall along the slots; image 0 has 128 to 255 slots and image 1 runs from there to the replica's last slot, unused slots included. `valid_counts`: some replica uses all its slots. `vector_params`: rows 0, 5, 6 and 9 of each block are positive.
All inputs are finite; a program needn't handle non-finite values.
Results may differ from the reference program's by a relative error of at most 0.012.
The reference program's roundings to bfloat16 on the way count: a program that leaves them out, or rounds other values in their place, can miss the bound.
Values may be sent and summed in bfloat16 or wider, within the bound.
No kernel may reach another device: no remote copies, remote signals or barrier semaphores. Data moves between devices by JAX's collectives and lax.ppermute only.
A program may use at most 128 MiB of HBM per device.

```python
import math
import jax
import jax.numpy as jnp
import numpy as np
from jax import lax

D = 1024
HEADS = 16
HD = 64
FF = 4096
LAYERS = 2
VEC = 14
STEP = 10
TOK_DEV = 128
TOK_REP = 512
TOKENS = 16384
N_DP = 32
N_MP = 4


def pack_bounds(key):
    count_key, full_key, first_key = jax.random.split(key, 3)
    last_start = (N_MP - 1) * TOK_DEV
    counts = jax.random.randint(count_key, (N_DP,), last_start + TOK_DEV // 2, TOK_REP + 1)
    full_replica = jax.random.randint(full_key, (), 0, N_DP)
    counts = jnp.where(jnp.arange(N_DP) == full_replica, TOK_REP, counts).astype(jnp.int32)
    first_end = jax.random.randint(first_key, (N_DP,), TOK_DEV, 2 * TOK_DEV)
    return (counts, first_end)


def draw_image_ids(key, part):
    counts, first_end = pack_bounds(key)
    position = jnp.arange(TOK_REP, dtype=jnp.int32)[None, :]
    return (position >= first_end[:, None]).astype(jnp.int32)


def draw_valid_counts(key, part):
    counts, first_end = pack_bounds(key)
    return counts


def draw_vector_params(key, part):
    key = jax.random.fold_in(key, 5)
    gain_key, shift_key = jax.random.split(key)
    is_gain = jnp.asarray(np.array([1, 0, 0, 0, 0, 1, 1, 0, 0, 1] + [0] * (VEC - 10), dtype=np.float32))
    gains = jax.random.uniform(gain_key, (LAYERS, VEC, D), jnp.float32, 0.5, 1.5)
    shifts = jnp.clip(0.5 * jax.random.normal(shift_key, (LAYERS, VEC, D), jnp.float32), -2.0, 2.0)
    return jnp.where(is_gain[None, :, None] > 0.5, gains, shifts)


def steps_of(own_key, dims, shards, smallest, largest):
    loudness, own = 1.0, jax.random.fold_in(own_key, 6)
    for dim, shards_of in shards:
        draws = jnp.exp(jax.random.uniform(jax.random.fold_in(own, dim), (shards_of,), jnp.float32, smallest / len(shards), largest / len(shards)))
        loudness = loudness * jnp.repeat(draws, dims[dim] // shards_of).reshape([-1 if axis == dim else 1 for axis in range(len(dims))])
    return loudness


def normal_values(stream_key, extent, scale, most, cuts=(), kind=jnp.bfloat16):
    entries = scale * jax.random.normal(stream_key, extent, jnp.float32)
    if cuts:
        entries = entries * steps_of(stream_key, extent, cuts, -0.22, 0.18)
    return jnp.clip(entries, -most, most).astype(kind)


def setup_inputs(seed: int = 0) -> dict:
    key_of = jax.random.split(jax.random.key(seed), 20)
    return {
        "tokens": normal_values(key_of[0], (TOKENS, D), 1.0, 6.0, ((0, 128),)),
        "cotangent": normal_values(key_of[1], (TOKENS, D), 1.0, 6.0, ((0, 128),)),
        "image_ids": draw_image_ids(jax.random.fold_in(key_of[19], 71), 0),
        "valid_counts": draw_valid_counts(jax.random.fold_in(key_of[19], 71), 0),
        "attend_weight": normal_values(key_of[4], (LAYERS, D, 3, D), D ** -0.5, 0.1875, ((1, 32), (3, 4)), jnp.float32),
        "output_weight": normal_values(key_of[5], (LAYERS, D, D), (D // 16) ** -0.5, 0.75, ((1, 4), (2, 32)), jnp.float32),
        "expand_weight": normal_values(key_of[6], (LAYERS, D, FF), D ** -0.5, 0.1875, ((1, 32), (2, 4)), jnp.float32),
        "reduce_weight": normal_values(key_of[7], (LAYERS, FF, D), FF ** -0.5, 0.09375, ((1, 4), (2, 32)), jnp.float32),
        "vector_params": draw_vector_params(jax.random.fold_in(key_of[19], 71), 0),
        "attend_first": normal_values(key_of[9], (LAYERS, D, 3, D), (0.055 * TOKENS ** 0.5), 40.0, ((1, 32), (3, 4)), jnp.float32),
        "output_first": normal_values(key_of[10], (LAYERS, D, D), (0.0275 * TOKENS ** 0.5), 20.0, ((1, 4), (2, 32)), jnp.float32),
        "expand_first": normal_values(key_of[11], (LAYERS, D, FF), (0.033 * TOKENS ** 0.5), 24.0, ((1, 32), (2, 4)), jnp.float32),
        "reduce_first": normal_values(key_of[12], (LAYERS, FF, D), (0.072 * TOKENS ** 0.5), 56.0, ((1, 4), (2, 32)), jnp.float32),
        "vector_first": normal_values(key_of[13], (LAYERS, VEC, D), (0.066 * TOKENS ** 0.5), 48.0, ((2, 32),), jnp.float32),
        "attend_second": jnp.clip(jnp.exp(math.log(16.384) - 1.3862944 * jax.random.uniform(key_of[14], (LAYERS, D, 3, D), jnp.float32) ** steps_of(key_of[14], (LAYERS, D, 3, D), ((1, 32), (3, 4)), -0.2, 0.2)), 4.096, 16.384),
        "output_second": jnp.clip(jnp.exp(math.log(4.096) - 1.3862944 * jax.random.uniform(key_of[15], (LAYERS, D, D), jnp.float32) ** steps_of(key_of[15], (LAYERS, D, D), ((1, 4), (2, 32)), -0.2, 0.2)), 1.024, 4.096),
        "expand_second": jnp.clip(jnp.exp(math.log(5.89824) - 1.3862944 * jax.random.uniform(key_of[16], (LAYERS, D, FF), jnp.float32) ** steps_of(key_of[16], (LAYERS, D, FF), ((1, 32), (2, 4)), -0.2, 0.2)), 1.47456, 5.89824),
        "reduce_second": jnp.clip(jnp.exp(math.log(27.8528) - 1.39812884 * jax.random.uniform(key_of[17], (LAYERS, FF, D), jnp.float32) ** steps_of(key_of[17], (LAYERS, FF, D), ((1, 4), (2, 32)), -0.2, 0.2)), 6.88128, 27.8528),
        "vector_second": jnp.clip(jnp.exp(math.log(262.144) - 1.3862944 * jax.random.uniform(key_of[18], (LAYERS, VEC, D), jnp.float32) ** steps_of(key_of[18], (LAYERS, VEC, D), ((2, 32),), -0.2, 0.2)), 65.536, 262.144),
    }


@jax.custom_vjp
def low(v):
    return lax.optimization_barrier(v.astype(jnp.bfloat16)).astype(jnp.float32)

@jax.custom_vjp
def low_back(v):
    return v

def low_keep(v):
    return (low(v), None)

def low_pass(kept, grad):
    return (grad,)

def back_keep(v):
    return (v, None)

def back_low(kept, grad):
    return (low(grad),)
low.defvjp(low_keep, low_pass)
low_back.defvjp(back_keep, back_low)

def matmul(left, right):
    return jnp.dot(left, right, precision=lax.Precision.HIGHEST, preferred_element_type=jnp.float32)

def norm_rows(values, gain, shift):
    centre = lax.optimization_barrier(jnp.mean(values, axis=-1, keepdims=True))
    centred = values - centre
    spread = lax.optimization_barrier(jnp.mean(centred * centred, axis=-1, keepdims=True))
    return centred * lax.rsqrt(spread + 1e-06) * gain + shift

def replica_attention(packed):
    triple, image_row, live_count = packed
    heads_all = triple.reshape(TOK_REP, 3, HEADS, HD)
    position = jnp.arange(TOK_REP, dtype=jnp.int32)
    allowed = (image_row[:, None] == image_row[None, :]) & ((position[None, :] < live_count) | (position[:, None] == position[None, :]))
    scores = jnp.einsum('qhd,khd->hqk', heads_all[:, 0], heads_all[:, 1], precision=lax.Precision.HIGHEST) * HD ** (-0.5)
    scores = low_back(jnp.where(allowed[None], scores, -1e+30))
    top_score = lax.optimization_barrier(jnp.max(scores, axis=-1, keepdims=True))
    weights = jnp.exp(scores - top_score)
    probs = low(weights / lax.optimization_barrier(jnp.sum(weights, axis=-1, keepdims=True)))
    mixed = jnp.einsum('hqk,khd->qhd', probs, heads_all[:, 2], precision=lax.Precision.HIGHEST)
    return mixed.reshape(TOK_REP, D)

def forward(input_rows, attend_all, output_all, expand_all, shrink_all, vector_all, image_ids, valid_counts):
    attend_all = low(attend_all)
    output_all = low(output_all)
    expand_all = low(expand_all)
    shrink_all = low(shrink_all)
    vector_all = low(vector_all)
    attend_block = jax.checkpoint(replica_attention)
    hidden = input_rows
    for layer_index in range(LAYERS):
        params = vector_all[layer_index]
        normed = low(norm_rows(hidden, params[0], params[1]))
        bias = jnp.stack([params[2], jnp.zeros_like(params[2]), params[3]])
        triple = matmul(normed, attend_all[layer_index].reshape(D, 3 * D)).reshape(TOKENS, 3, D) + bias[None]
        triple = low(low_back(triple))
        mixed = lax.map(attend_block, (triple.reshape(N_DP, TOK_REP, 3, D), image_ids, valid_counts))
        mixed = low(low_back(mixed.reshape(TOKENS, D)))
        branch = low_back(matmul(mixed, output_all[layer_index]) + params[4])
        middle = hidden + params[5] * branch
        normed_two = low(norm_rows(middle, params[6], params[7]))
        inner = low_back(matmul(normed_two, expand_all[layer_index]) + params[10:].reshape(FF))
        active = low(jax.nn.gelu(inner, approximate=False))
        second_branch = low_back(matmul(active, shrink_all[layer_index]) + params[8])
        hidden = middle + params[9] * second_branch
    return hidden

def adamw(weight, first, second, grad, rate, decay):
    first_new = 0.9 * first + 0.1 * grad
    second_new = 0.999 * second + 0.001 * grad * grad
    scaled = first_new / (1.0 - 0.9 ** STEP) / (jnp.sqrt(second_new / (1.0 - 0.999 ** STEP)) + 1e-08)
    return (weight - rate * (scaled + decay * weight), first_new, second_new)

def reference(tokens, cotangent, image_ids, valid_counts, attend_weight, output_weight, expand_weight, reduce_weight, vector_params, attend_first, output_first, expand_first, reduce_first, vector_first, attend_second, output_second, expand_second, reduce_second, vector_second):
    input_rows = tokens.astype(jnp.float32)
    position = jnp.arange(TOK_REP, dtype=jnp.int32)
    valid = (position[None, :] < valid_counts[:, None]).astype(jnp.float32).reshape(TOKENS, 1)
    seed_grad = cotangent.astype(jnp.float32) * valid

    def run(rows_in, attend_all, output_all, expand_all, shrink_all, vector_all):
        return forward(rows_in, attend_all, output_all, expand_all, shrink_all, vector_all, image_ids, valid_counts)
    block_out, pull = jax.vjp(run, input_rows, attend_weight, output_weight, expand_weight, reduce_weight, vector_params)
    grads = pull(seed_grad)
    weights = (attend_weight, output_weight, expand_weight, reduce_weight, vector_params)
    firsts = (attend_first, output_first, expand_first, reduce_first, vector_first)
    seconds = (attend_second, output_second, expand_second, reduce_second, vector_second)
    rates = (D ** (-0.5), 4.0 * D ** (-0.5), D ** (-0.5), FF ** (-0.5), 0.25)
    decays = (0.05, 0.05, 0.05, 0.05, 0.0)
    results = [adamw(weights[index], firsts[index], seconds[index], grads[index + 1], rates[index], decays[index]) for index in range(5)]
    return (block_out, grads[0], results[0][0], results[1][0], results[2][0], results[3][0], results[4][0], results[0][1], results[1][1], results[2][1], results[3][1], results[4][1], results[0][2], results[1][2], results[2][2], results[3][2], results[4][2])
```

```python
import jax
import jax.numpy as jnp
from jax import lax
from jax.sharding import Mesh, PartitionSpec as P

D = 1024
HD = 64
FF = 4096
LAYERS = 2
STEP = 10
BF = jnp.bfloat16
F32 = jnp.float32
DP = ("z", "yl", "x")
MP = ("yh", "core")


def swap(values, axis):
    return lax.ppermute(values, axis, [(0, 1), (1, 0)])


def to_inner(values):
    lead = values.shape[:-1]
    return jnp.swapaxes(values.reshape(lead + (4, 2, 4, 32)), -3, -2).reshape(lead + (D,))


def to_outer(values):
    lead = values.shape[:-1]
    return jnp.swapaxes(values.reshape(lead + (4, 4, 2, 32)), -3, -2).reshape(lead + (D,))


def gather_rows(values):
    across = swap(values, "yh")
    mate = swap(values, "core")
    diagonal = swap(across, "core")
    return jnp.concatenate([values, mate, across, diagonal], axis=0)


def scatter_rows(partial):
    rows = partial.shape[0] // 4
    own, mate, across, diagonal = (partial[k * rows : (k + 1) * rows] for k in range(4))
    chip = across + swap(diagonal, "core")
    far = swap(chip.astype(BF), "yh").astype(F32)
    return own + swap(mate, "core") + far


def dot(left, right):
    return jnp.dot(left, right, preferred_element_type=F32)


def dot_t(left, right):
    return jnp.einsum("rf,df->rd", left, right, preferred_element_type=F32)


def wgrad(left, right):
    return jnp.einsum("rd,rf->df", left, right, preferred_element_type=F32)


def norm_parts(values):
    centre = jnp.mean(values, axis=-1, keepdims=True)
    centred = values - centre
    spread = jnp.mean(centred * centred, axis=-1, keepdims=True)
    inverse = lax.rsqrt(spread + 1e-06)
    return centred * inverse, inverse


def norm_back(normal, inverse, gain, grad):
    scaled = grad * gain
    middle = jnp.mean(scaled, axis=-1, keepdims=True)
    slope = jnp.mean(scaled * normal, axis=-1, keepdims=True)
    return (
        (scaled - middle - normal * slope) * inverse,
        jnp.sum(grad * normal, axis=0),
        jnp.sum(grad, axis=0),
    )


def split_heads(triple):
    rows = triple.shape[0]
    parts = triple.reshape(rows, 3, -1, HD)
    return parts[:, 0], parts[:, 1], parts[:, 2]


def attention_forward(triple, allowed):
    query, key, value = split_heads(triple)
    scores = jnp.einsum("qhd,khd->hqk", query, key, preferred_element_type=F32) * HD ** (-0.5)
    scores = jnp.where(allowed[None], scores, -1e30)
    top_score = jnp.max(scores, axis=-1, keepdims=True)
    weights = jnp.exp(scores - top_score)
    total = jnp.sum(weights, axis=-1, keepdims=True)
    probs = (weights / total).astype(BF)
    mixed = jnp.einsum("hqk,khd->qhd", probs, value, preferred_element_type=F32)
    return mixed.astype(BF).reshape(triple.shape[0], -1), top_score + jnp.log(total)


def attention_backward(triple, log_total, mixed_grad, allowed):
    rows = triple.shape[0]
    query, key, value = split_heads(triple)
    grads = mixed_grad.reshape(rows, -1, HD)
    scale = HD ** (-0.5)
    scores = jnp.einsum("qhd,khd->hqk", query, key, preferred_element_type=F32) * scale
    scores = jnp.where(allowed[None], scores, -1e30)
    probs = jnp.exp(scores - log_total)
    prob_grad = jnp.einsum("qhd,khd->hqk", grads, value, preferred_element_type=F32)
    centre = jnp.sum(probs * prob_grad, axis=-1, keepdims=True)
    score_grad = (probs * (prob_grad - centre)).astype(BF)
    query_grad = jnp.einsum("hqk,khd->qhd", score_grad, key, preferred_element_type=F32) * scale
    key_grad = jnp.einsum("hqk,qhd->khd", score_grad, query, preferred_element_type=F32) * scale
    value_grad = jnp.einsum("hqk,qhd->khd", probs.astype(BF), grads, preferred_element_type=F32)
    stacked = jnp.stack([query_grad, key_grad, value_grad], axis=1)
    return stacked.reshape(rows, -1).astype(BF)


def adamw(weight, first, second, grad, rate, decay):
    first_new = 0.9 * first + 0.1 * grad
    second_new = 0.999 * second + 0.001 * grad * grad
    scaled = first_new / (1.0 - 0.9**STEP) / (jnp.sqrt(second_new / (1.0 - 0.999**STEP)) + 1e-08)
    return (weight - rate * (scaled + decay * weight), first_new, second_new)


def gather_pack(pack, low_row):
    other = swap(pack, "yl")
    pair = jnp.where(
        low_row == 0, jnp.concatenate([pack, other], 0), jnp.concatenate([other, pack], 0)
    )
    return lax.all_gather(pair, ("z", "x"), axis=0, tiled=True)


def scatter_pack(pack, low_row):
    pair = lax.psum_scatter(pack, ("z", "x"), scatter_dimension=0, tiled=True)
    rows = pair.shape[0] // 2
    own = lax.dynamic_slice_in_dim(pair, low_row * rows, rows, 0)
    other = lax.dynamic_slice_in_dim(pair, (1 - low_row) * rows, rows, 0)
    return own + swap(other, "yl")


def per_device(
    tokens,
    cotangent,
    image_ids,
    valid_counts,
    attend_weight,
    output_weight,
    expand_weight,
    reduce_weight,
    vector_params,
    attend_first,
    output_first,
    expand_first,
    reduce_first,
    vector_first,
    attend_second,
    output_second,
    expand_second,
    reduce_second,
    vector_second,
):
    me = lax.axis_index(MP)
    low_row = lax.axis_index("yl")
    rows = tokens.shape[0]
    width = attend_weight.shape[-1]
    hidden_width = expand_weight.shape[-1]
    feats = attend_weight.shape[1]
    live_count = valid_counts[0]

    attend_low = attend_weight.astype(BF).reshape(LAYERS, feats, 3 * width)
    output_low = jnp.swapaxes(output_weight.astype(BF), 1, 2)
    expand_low = expand_weight.astype(BF)
    reduce_low = jnp.swapaxes(reduce_weight.astype(BF), 1, 2)
    vector_rows = vector_params.shape[1]
    vector_low = vector_params.astype(BF).reshape(LAYERS * vector_rows, feats).T
    vector_low = jnp.pad(vector_low, ((0, 0), (0, 128 - LAYERS * vector_rows)))
    first_pack = gather_pack(jnp.concatenate([attend_low[0], vector_low], 1), low_row)
    second_pack = gather_pack(
        jnp.concatenate([output_low[0], expand_low[0], reduce_low[0]], 1), low_row
    )
    third_pack = gather_pack(
        jnp.concatenate([attend_low[1], output_low[1], expand_low[1], reduce_low[1]], 1), low_row
    )
    cuts = (3 * width, 4 * width, 4 * width + hidden_width, 4 * width + 2 * hidden_width)
    weights_of = (
        (
            first_pack[:, : cuts[0]],
            second_pack[:, : cuts[1] - cuts[0]],
            second_pack[:, cuts[1] - cuts[0] : cuts[2] - cuts[0]],
            second_pack[:, cuts[2] - cuts[0] :],
        ),
        (
            third_pack[:, : cuts[0]],
            third_pack[:, cuts[0] : cuts[1]],
            third_pack[:, cuts[1] : cuts[2]],
            third_pack[:, cuts[2] :],
        ),
    )
    vectors = first_pack[:, cuts[0] : cuts[0] + LAYERS * vector_rows].T.astype(F32)
    vectors_outer = to_outer(vectors)

    image_parts = image_ids[0].reshape(4, rows)
    image_row = jnp.concatenate([image_parts[me ^ k] for k in range(4)])
    position = jnp.concatenate(
        [(me ^ k) * rows + jnp.arange(rows, dtype=jnp.int32) for k in range(4)]
    )
    allowed = (image_row[:, None] == image_row[None, :]) & (
        (position[None, :] < live_count) | (position[:, None] == position[None, :])
    )

    hidden = to_inner(tokens).astype(F32)
    saved = []
    for layer in range(LAYERS):
        attend_full, output_full, expand_full, reduce_full = weights_of[layer]
        params = vectors[layer * vector_rows : (layer + 1) * vector_rows]
        outer = vectors_outer[layer * vector_rows : (layer + 1) * vector_rows]
        normal, inverse = norm_parts(hidden)
        normed_all = gather_rows((normal * params[0] + params[1]).astype(BF))
        bias = jnp.concatenate(
            [
                lax.dynamic_slice_in_dim(outer[2], me * width, width, 0),
                jnp.zeros((width,), F32),
                lax.dynamic_slice_in_dim(outer[3], me * width, width, 0),
            ]
        )
        triple = (dot(normed_all, attend_full) + bias).astype(BF)
        mixed, log_total = attention_forward(triple, allowed)
        branch = scatter_rows(dot_t(mixed, output_full)) + params[4]
        middle = hidden + params[5] * branch
        normal_two, inverse_two = norm_parts(middle)
        normed_two_all = gather_rows((normal_two * params[6] + params[7]).astype(BF))
        inner_bias = lax.dynamic_index_in_dim(outer[10:], me, 0, keepdims=False)
        inner = dot(normed_two_all, expand_full) + inner_bias
        active = jax.nn.gelu(inner, approximate=False).astype(BF)
        second_branch = scatter_rows(dot_t(active, reduce_full)) + params[8]
        saved.append(
            (
                normal,
                inverse,
                normed_all,
                triple,
                log_total,
                mixed,
                branch,
                normal_two,
                inverse_two,
                normed_two_all,
                inner,
                active,
                second_branch,
            )
        )
        hidden = middle + params[9] * second_branch

    own_position = me * rows + jnp.arange(rows, dtype=jnp.int32)
    grad_hidden = (
        to_inner(cotangent).astype(F32) * (own_position < live_count).astype(F32)[:, None]
    )
    matrix_grads = [None] * LAYERS
    vector_grads = [None] * LAYERS
    for layer in range(LAYERS - 1, -1, -1):
        attend_full, output_full, expand_full, reduce_full = weights_of[layer]
        params = vectors[layer * vector_rows : (layer + 1) * vector_rows]
        (
            normal,
            inverse,
            normed_all,
            triple,
            log_total,
            mixed,
            branch,
            normal_two,
            inverse_two,
            normed_two_all,
            inner,
            active,
            second_branch,
        ) = saved[layer]
        reduce_rows = (params[9] * grad_hidden).astype(BF)
        scale_two_grad = jnp.sum(grad_hidden * second_branch, axis=0)
        shift_out_grad = jnp.sum(reduce_rows.astype(F32), axis=0)
        reduce_all = gather_rows(reduce_rows)
        reduce_wgrad = wgrad(reduce_all, active)
        active_grad = dot(reduce_all, reduce_full)
        gelu_slope = 0.5 * (1.0 + lax.erf(inner * 0.5**0.5)) + inner * jnp.exp(
            -0.5 * inner * inner
        ) * (0.5 / jnp.pi) ** 0.5
        inner_grad = (active_grad * gelu_slope).astype(BF)
        inner_bias_grad = jnp.sum(inner_grad.astype(F32), axis=0)
        expand_wgrad = wgrad(normed_two_all, inner_grad)
        normed_two_grad = scatter_rows(dot_t(inner_grad, expand_full))
        middle_extra, gain_two_grad, shift_two_grad = norm_back(
            normal_two, inverse_two, params[6], normed_two_grad
        )
        grad_middle = grad_hidden + middle_extra
        branch_rows = (params[5] * grad_middle).astype(BF)
        scale_one_grad = jnp.sum(grad_middle * branch, axis=0)
        shift_att_grad = jnp.sum(branch_rows.astype(F32), axis=0)
        branch_all = gather_rows(branch_rows)
        output_wgrad = wgrad(branch_all, mixed)
        mixed_grad = dot(branch_all, output_full).astype(BF)
        triple_grad = attention_backward(triple, log_total, mixed_grad, allowed)
        triple_sums = jnp.sum(triple_grad.astype(F32), axis=0).reshape(3, width)
        attend_wgrad = wgrad(normed_all, triple_grad)
        normed_grad = scatter_rows(dot_t(triple_grad, attend_full))
        hidden_extra, gain_one_grad, shift_one_grad = norm_back(
            normal, inverse, params[0], normed_grad
        )
        grad_hidden = grad_middle + hidden_extra
        matrix_grads[layer] = (attend_wgrad, output_wgrad, expand_wgrad, reduce_wgrad)

        def place(values, total):
            return lax.dynamic_update_slice_in_dim(
                jnp.zeros((total,), F32), values, me * values.shape[0], 0
            )

        outer_rows = to_inner(
            jnp.concatenate(
                [
                    place(triple_sums[0], D)[None],
                    place(triple_sums[2], D)[None],
                    place(inner_bias_grad, FF).reshape(-1, D),
                ]
            )
        )
        vector_grads[layer] = jnp.concatenate(
            [
                gain_one_grad[None],
                shift_one_grad[None],
                outer_rows[:2],
                shift_att_grad[None],
                scale_one_grad[None],
                gain_two_grad[None],
                shift_two_grad[None],
                shift_out_grad[None],
                scale_two_grad[None],
                outer_rows[2:],
            ]
        )

    early = scatter_pack(jnp.concatenate(matrix_grads[1][2:], 1), low_row)
    later = scatter_pack(jnp.concatenate(matrix_grads[1][:2] + matrix_grads[0][2:], 1), low_row)
    vector_all = jnp.concatenate(vector_grads, 0)
    vector_high = lax.reduce_precision(vector_all, 8, 7)
    vector_rest = vector_all - vector_high
    vector_cols = jnp.pad(
        jnp.concatenate([vector_high, vector_rest], 0).T,
        ((0, 0), (0, 128 - 2 * LAYERS * vector_rows)),
    ).astype(BF)
    last = jnp.concatenate(
        [matrix_grads[0][0].astype(BF), matrix_grads[0][1].astype(BF), vector_cols], 1
    )
    last = lax.all_to_all(last, ("z", "x", "yl"), 0, 0, tiled=True)
    last = jnp.sum(last.reshape(-1, feats, last.shape[1]).astype(F32), axis=0)
    vector_sum = (
        last[:, cuts[1] : cuts[1] + LAYERS * vector_rows]
        + last[:, cuts[1] + LAYERS * vector_rows : cuts[1] + 2 * LAYERS * vector_rows]
    )
    vector_sum = vector_sum + swap(vector_sum, "core")
    vector_sum = vector_sum + swap(vector_sum, "yh")
    attend_sum = jnp.stack([last[:, : cuts[0]], later[:, : cuts[0]]])
    output_sum = jnp.stack([last[:, cuts[0] : cuts[1]], later[:, cuts[0] : cuts[1]]])
    expand_sum = jnp.stack(
        [later[:, cuts[1] : cuts[2]], early[:, :hidden_width]]
    )
    reduce_sum = jnp.stack([later[:, cuts[2] :], early[:, hidden_width:]])
    reduced = (
        attend_sum.reshape(attend_weight.shape),
        jnp.swapaxes(output_sum, 1, 2),
        expand_sum,
        jnp.swapaxes(reduce_sum, 1, 2),
        vector_sum.T.reshape(vector_params.shape),
    )
    weights = (attend_weight, output_weight, expand_weight, reduce_weight, vector_params)
    firsts = (attend_first, output_first, expand_first, reduce_first, vector_first)
    seconds = (attend_second, output_second, expand_second, reduce_second, vector_second)
    rates = (D ** (-0.5), 4.0 * D ** (-0.5), D ** (-0.5), FF ** (-0.5), 0.25)
    decays = (0.05, 0.05, 0.05, 0.05, 0.0)
    results = [
        adamw(
            weights[member],
            firsts[member],
            seconds[member],
            reduced[member],
            rates[member],
            decays[member],
        )
        for member in range(5)
    ]
    return (to_outer(hidden), to_outer(grad_hidden)) + tuple(
        results[member][kind] for kind in range(3) for member in range(5)
    )


def solution(mesh):
    fine = Mesh(mesh.devices.reshape(4, 2, 4, 2, 2), DP + MP)
    rows = P(DP + MP, None)
    attend = P(None, DP, None, MP)
    output = P(None, MP, DP)
    expand = P(None, DP, MP)
    vector = P(None, None, DP)
    params = (attend, output, expand, output, vector)
    return jax.shard_map(
        per_device,
        mesh=fine,
        in_specs=(rows, rows, P(DP, None), P(DP)) + params * 3,
        out_specs=(rows, rows) + params * 3,
        check_vma=False,
    )
```

```python
import jax
import jax.numpy as jnp
from jax import lax
from jax.experimental import pallas as pl
from jax.experimental.pallas import tpu as pltpu
from jax.sharding import Mesh, PartitionSpec as P

D = 1024
HD = 64
FF = 4096
LAYERS = 2
STEP = 10
BF = jnp.bfloat16
F32 = jnp.float32
DP = ("z", "yl", "x")
MP = ("yh", "core")


def swap(values, axis):
    return lax.ppermute(values, axis, [(0, 1), (1, 0)])


def to_inner(values):
    lead = values.shape[:-1]
    return jnp.swapaxes(values.reshape(lead + (4, 2, 4, 32)), -3, -2).reshape(lead + (D,))


def to_outer(values):
    lead = values.shape[:-1]
    return jnp.swapaxes(values.reshape(lead + (4, 4, 2, 32)), -3, -2).reshape(lead + (D,))


def gather_rows(values, work=None):
    across = swap(values, "yh")
    near = jnp.concatenate([values, swap(values, "core")], axis=0)
    done = None
    if work is not None:
        across, done = lax.optimization_barrier((across, work(near)))
    far = jnp.concatenate([across, swap(across, "core")], axis=0)
    return near, far, done


def scatter_rows(near, far, work=None):
    rows = near.shape[0] // 2
    chip = far[:rows] + swap(far[rows:], "core")
    other = swap(chip.astype(BF), "yh")
    if work is not None:
        other, work = lax.optimization_barrier((other, work))
    return near[:rows] + swap(near[rows:], "core") + other.astype(F32), work


def dot(left, right):
    return jnp.dot(left, right, preferred_element_type=F32)


def dot_t(left, right):
    return jnp.einsum("rf,df->rd", left, right, preferred_element_type=F32)


def dot_first(left, right):
    return lax.dot_general(left, right, (((0,), (0,)), ((), ())), preferred_element_type=F32)


def dot_last(left, right):
    return lax.dot_general(left, right, (((1,), (1,)), ((), ())), preferred_element_type=F32)


def kernel_cost(flops, size, transcendentals=0):
    return pl.CostEstimate(flops=flops, bytes_accessed=size, transcendentals=transcendentals)


def weight_grads(sums, out_type, vectors=()):
    feats = sums[0][0][0].shape[1]
    widths = [pairs[0][1].shape[1] for pairs in sums]
    total = sum(widths) + (128 if vectors else 0)
    count = len(vectors)
    block = 256
    specs, operands = [], []
    for pairs in sums:
        for left, right in pairs:
            specs.append(pl.BlockSpec((left.shape[0], block), lambda i: (0, i)))
            specs.append(pl.BlockSpec(right.shape, lambda i: (0, 0)))
            operands += [left, right]
    for values in vectors:
        specs.append(pl.BlockSpec((1, block), lambda i: (0, i)))
        operands.append(values.reshape(1, feats))

    def kernel(*refs):
        refs = list(refs)
        table = refs.pop() if vectors else None
        out_ref = refs.pop()
        start = 0
        for width, pairs in zip(widths, sums):
            acc = None
            for _ in pairs:
                left, right = refs.pop(0), refs.pop(0)
                part = dot_first(left[...], right[...])
                acc = part if acc is None else acc + part
            out_ref[:, start : start + width] = acc.astype(out_type)
            start += width
        if vectors:
            table[...] = jnp.zeros_like(table)
            for index, row in enumerate(refs):
                values = row[...]
                high = values.astype(BF).astype(F32)
                table[index : index + 1, :] = high
                table[count + index : count + index + 1, :] = values - high
            spots = lax.broadcasted_iota(jnp.int32, (128, 128), 0)
            eye = (spots == lax.broadcasted_iota(jnp.int32, (128, 128), 1)).astype(BF)
            out_ref[:, start:] = dot_first(table[...].astype(BF), eye).astype(out_type)

    depth = sum(left.shape[0] for left, _ in sums[0])
    return pl.pallas_call(
        kernel,
        grid=(feats // block,),
        in_specs=specs,
        out_specs=pl.BlockSpec((block, total), lambda i: (i, 0)),
        out_shape=jax.ShapeDtypeStruct((feats, total), out_type),
        scratch_shapes=[pltpu.VMEM((128, block), F32)] if vectors else [],
        compiler_params=pltpu.CompilerParams(vmem_limit_bytes=40 * 2**20),
        cost_estimate=kernel_cost(2 * depth * feats * total, feats * total * 4),
    )(*operands)


def hidden_forward(normed, pack, bias):
    rows, feats = normed.shape
    width = bias.shape[0]
    block = 256
    steps = width // block

    def kernel(normed_ref, expand_ref, reduce_ref, bias_ref, active_ref, slope_ref, part_ref):
        inner = dot(normed_ref[...], expand_ref[...]) + bias_ref[...]
        half = 0.5 * (1.0 + lax.erf(inner * 0.5**0.5))
        active = (inner * half).astype(BF)
        active_ref[...] = active
        slope_ref[...] = half + inner * jnp.exp(-0.5 * inner * inner) * (0.5 / jnp.pi) ** 0.5
        part = dot_last(active, reduce_ref[...])

        @pl.when(pl.program_id(0) == 0)
        def _():
            part_ref[...] = part

        @pl.when(pl.program_id(0) > 0)
        def _():
            part_ref[...] += part

    chunk = pl.BlockSpec((rows, block), lambda i: (0, i))
    whole = pl.BlockSpec((rows, feats), lambda i: (0, 0))
    return pl.pallas_call(
        kernel,
        grid=(steps,),
        in_specs=[
            whole,
            pl.BlockSpec((feats, block), lambda i: (0, i)),
            pl.BlockSpec((feats, block), lambda i: (0, i + steps)),
            pl.BlockSpec((1, block), lambda i: (0, i)),
        ],
        out_specs=[chunk, chunk, whole],
        out_shape=[
            jax.ShapeDtypeStruct((rows, width), BF),
            jax.ShapeDtypeStruct((rows, width), F32),
            jax.ShapeDtypeStruct((rows, feats), F32),
        ],
        compiler_params=pltpu.CompilerParams(vmem_limit_bytes=32 * 2**20),
        cost_estimate=kernel_cost(8 * rows * feats * width, 8 * 2**20, 2 * rows * width),
    )(normed, pack, pack, bias.reshape(1, width))


def hidden_backward(grads, slope, pack):
    rows, feats = grads.shape
    width = slope.shape[1]
    block = 256
    steps = width // block

    def kernel(grads_ref, slope_ref, expand_ref, reduce_ref, inner_ref, bias_ref, part_ref):
        inner_grad = (dot(grads_ref[...], reduce_ref[...]) * slope_ref[...]).astype(BF)
        inner_ref[...] = inner_grad
        bias_ref[...] = jnp.sum(inner_grad.astype(F32), axis=0, keepdims=True)
        part = dot_last(inner_grad, expand_ref[...])

        @pl.when(pl.program_id(0) == 0)
        def _():
            part_ref[...] = part

        @pl.when(pl.program_id(0) > 0)
        def _():
            part_ref[...] += part

    chunk = pl.BlockSpec((rows, block), lambda i: (0, i))
    whole = pl.BlockSpec((rows, feats), lambda i: (0, 0))
    return pl.pallas_call(
        kernel,
        grid=(steps,),
        in_specs=[
            whole,
            chunk,
            pl.BlockSpec((feats, block), lambda i: (0, i)),
            pl.BlockSpec((feats, block), lambda i: (0, i + steps)),
        ],
        out_specs=[chunk, pl.BlockSpec((1, block), lambda i: (0, i)), whole],
        out_shape=[
            jax.ShapeDtypeStruct((rows, width), BF),
            jax.ShapeDtypeStruct((1, width), F32),
            jax.ShapeDtypeStruct((rows, feats), F32),
        ],
        compiler_params=pltpu.CompilerParams(vmem_limit_bytes=32 * 2**20),
        cost_estimate=kernel_cost(6 * rows * feats * width, 8 * 2**20),
    )(grads, slope, pack, pack)


def norm_parts(values):
    centre = jnp.mean(values, axis=-1, keepdims=True)
    centred = values - centre
    spread = jnp.mean(centred * centred, axis=-1, keepdims=True)
    inverse = lax.rsqrt(spread + 1e-06)
    return centred * inverse, inverse


def norm_back(normal, inverse, gain, grad):
    scaled = grad * gain
    middle = jnp.mean(scaled, axis=-1, keepdims=True)
    slope = jnp.mean(scaled * normal, axis=-1, keepdims=True)
    return (
        (scaled - middle - normal * slope) * inverse,
        jnp.sum(grad * normal, axis=0),
        jnp.sum(grad, axis=0),
    )


def split_heads(triple):
    rows = triple.shape[0]
    parts = triple.reshape(rows, 3, -1, HD)
    return parts[:, 0], parts[:, 1], parts[:, 2]


def attention_forward(triple, allowed):
    query, key, value = split_heads(triple)
    scores = jnp.einsum("qhd,khd->hqk", query, key, preferred_element_type=F32) * HD ** (-0.5)
    scores = jnp.where(allowed[None], scores, -1e30)
    top_score = jnp.max(scores, axis=-1, keepdims=True)
    weights = jnp.exp(scores - top_score)
    total = jnp.sum(weights, axis=-1, keepdims=True)
    probs = (weights / total).astype(BF)
    mixed = jnp.einsum("hqk,khd->qhd", probs, value, preferred_element_type=F32)
    return mixed.astype(BF).reshape(triple.shape[0], -1), top_score + jnp.log(total)


def attention_backward(triple, log_total, mixed_grad, allowed):
    rows = triple.shape[0]
    query, key, value = split_heads(triple)
    grads = mixed_grad.reshape(rows, -1, HD)
    scale = HD ** (-0.5)
    scores = jnp.einsum("qhd,khd->hqk", query, key, preferred_element_type=F32) * scale
    scores = jnp.where(allowed[None], scores, -1e30)
    probs = jnp.exp(scores - log_total)
    prob_grad = jnp.einsum("qhd,khd->hqk", grads, value, preferred_element_type=F32)
    centre = jnp.sum(probs * prob_grad, axis=-1, keepdims=True)
    score_grad = (probs * (prob_grad - centre)).astype(BF)
    query_grad = jnp.einsum("hqk,khd->qhd", score_grad, key, preferred_element_type=F32) * scale
    key_grad = jnp.einsum("hqk,qhd->khd", score_grad, query, preferred_element_type=F32) * scale
    value_grad = jnp.einsum("hqk,qhd->khd", probs.astype(BF), grads, preferred_element_type=F32)
    stacked = jnp.stack([query_grad, key_grad, value_grad], axis=1)
    return stacked.reshape(rows, -1).astype(BF)


def place(values, me):
    return lax.dynamic_update_slice_in_dim(
        jnp.zeros((D,), F32), values, me * values.shape[0], 0
    )


def adamw(weight, first, second, grad, rate, decay):
    first_new = 0.9 * first + 0.1 * grad
    second_new = 0.999 * second + 0.001 * grad * grad
    scaled = first_new / (1.0 - 0.9**STEP) / (jnp.sqrt(second_new / (1.0 - 0.999**STEP)) + 1e-08)
    return (weight - rate * (scaled + decay * weight), first_new, second_new)


def swap_pair(pack, low_row):
    other = swap(pack, "yl")
    return jnp.where(
        low_row == 0, jnp.concatenate([pack, other], 0), jnp.concatenate([other, pack], 0)
    )


def gather_pair(pair):
    return lax.all_gather(pair, ("z", "x"), axis=0, tiled=True)


def sum_pack(pack):
    return lax.psum_scatter(pack, ("z", "x"), scatter_dimension=0, tiled=True)


def sum_pair(pair, low_row):
    rows = pair.shape[0] // 2
    own = lax.dynamic_slice_in_dim(pair, low_row * rows, rows, 0)
    other = lax.dynamic_slice_in_dim(pair, (1 - low_row) * rows, rows, 0)
    return own.astype(F32) + swap(other, "yl").astype(F32)


def place(values, me):
    return lax.dynamic_update_slice_in_dim(
        jnp.zeros((D,), F32), values, me * values.shape[0], 0
    )


def adamw(weight, first, second, grad, rate, decay):
    first_new = 0.9 * first + 0.1 * grad
    second_new = 0.999 * second + 0.001 * grad * grad
    scaled = first_new / (1.0 - 0.9**STEP) / (jnp.sqrt(second_new / (1.0 - 0.999**STEP)) + 1e-08)
    return (weight - rate * (scaled + decay * weight), first_new, second_new)


def swap_pair(pack, low_row):
    other = swap(pack, "yl")
    return jnp.where(
        low_row == 0, jnp.concatenate([pack, other], 0), jnp.concatenate([other, pack], 0)
    )


def gather_pair(pair):
    return lax.all_gather(pair, ("z", "x"), axis=0, tiled=True)


def scatter_pack(pack, low_row):
    pair = lax.psum_scatter(pack, ("z", "x"), scatter_dimension=0, tiled=True)
    rows = pair.shape[0] // 2
    own = lax.dynamic_slice_in_dim(pair, low_row * rows, rows, 0)
    other = lax.dynamic_slice_in_dim(pair, (1 - low_row) * rows, rows, 0)
    return own.astype(F32) + swap(other, "yl").astype(F32)


def per_device(
    tokens,
    cotangent,
    image_ids,
    valid_counts,
    attend_weight,
    output_weight,
    expand_weight,
    reduce_weight,
    vector_params,
    attend_first,
    output_first,
    expand_first,
    reduce_first,
    vector_first,
    attend_second,
    output_second,
    expand_second,
    reduce_second,
    vector_second,
):
    me = lax.axis_index(MP)
    low_row = lax.axis_index("yl")
    rows = tokens.shape[0]
    width = attend_weight.shape[-1]
    hidden_width = expand_weight.shape[-1]
    feats = attend_weight.shape[1]
    live_count = valid_counts[0]

    attend_low = attend_weight.astype(BF).reshape(LAYERS, feats, 3 * width)
    output_low = jnp.swapaxes(output_weight.astype(BF), 1, 2)
    expand_low = expand_weight.astype(BF)
    reduce_low = jnp.swapaxes(reduce_weight.astype(BF), 1, 2)
    vector_rows = vector_params.shape[1]
    vector_low = vector_params.astype(BF).reshape(LAYERS * vector_rows, feats).T
    vector_low = jnp.pad(vector_low, ((0, 0), (0, 128 - LAYERS * vector_rows)))
    first_part = jnp.concatenate([attend_low[0], output_low[0], vector_low], 1)
    first_pack = lax.all_to_all(
        jnp.broadcast_to(first_part[None], (32,) + first_part.shape).reshape(
            -1, first_part.shape[1]
        ),
        ("z", "x", "yl"),
        0,
        0,
        tiled=True,
    )
    second_pack = gather_pair(
        swap_pair(jnp.concatenate([expand_low[0], reduce_low[0]], 1), low_row)
    )
    third_pair = swap_pair(
        jnp.concatenate([expand_low[1], reduce_low[1], attend_low[1], output_low[1]], 1), low_row
    )
    first_pack, third_pair = lax.optimization_barrier((first_pack, third_pair))
    third_pack = gather_pair(third_pair)
    cuts = (3 * width, 4 * width, 4 * width + hidden_width, 4 * width + 2 * hidden_width)
    packs = (
        (first_pack[:, : cuts[0]], first_pack[:, cuts[0] : cuts[1]], second_pack),
        (
            third_pack[:, 2 * hidden_width : 2 * hidden_width + cuts[0]],
            third_pack[:, 2 * hidden_width + cuts[0] :],
            third_pack,
        ),
    )
    vectors = lax.dot_general(
        jnp.eye(LAYERS * vector_rows, 128, dtype=BF),
        first_pack[:, cuts[1] :],
        (((1,), (1,)), ((), ())),
        preferred_element_type=F32,
    )
    vectors_outer = to_outer(vectors)

    image_parts = image_ids[0].reshape(4, rows)
    image_row = jnp.concatenate([image_parts[me ^ k] for k in range(4)])
    position = jnp.concatenate(
        [(me ^ k) * rows + jnp.arange(rows, dtype=jnp.int32) for k in range(4)]
    )
    allowed = (image_row[:, None] == image_row[None, :]) & (
        (position[None, :] < live_count) | (position[:, None] == position[None, :])
    )

    tokens_in = to_inner(tokens)
    tokens_all = jnp.concatenate(gather_rows(tokens_in)[:2], axis=0)
    first_normal, first_inverse = norm_parts(tokens_all.astype(F32))
    hidden = tokens_in.astype(F32)
    saved = []
    for layer in range(LAYERS):
        attend_full, output_full, hidden_pack = packs[layer]
        params = vectors[layer * vector_rows : (layer + 1) * vector_rows]
        outer = vectors_outer[layer * vector_rows : (layer + 1) * vector_rows]
        if layer == 0:
            normed_all = (first_normal * params[0] + params[1]).astype(BF)
            normal, inverse = first_normal[:rows], first_inverse[:rows]
        else:
            normal, inverse = norm_parts(hidden)
            normed_all = jnp.concatenate(
                gather_rows((normal * params[0] + params[1]).astype(BF))[:2], axis=0
            )
        bias = jnp.concatenate(
            [
                lax.dynamic_slice_in_dim(outer[2], me * width, width, 0),
                jnp.zeros((width,), F32),
                lax.dynamic_slice_in_dim(outer[3], me * width, width, 0),
            ]
        )
        triple = (dot(normed_all, attend_full) + bias).astype(BF)
        mixed, log_total = attention_forward(triple, allowed)
        branch_part = dot_t(mixed, output_full)
        branch = scatter_rows(branch_part[: 2 * rows], branch_part[2 * rows :])[0] + params[4]
        middle = hidden + params[5] * branch
        normal_two, inverse_two = norm_parts(middle)
        inner_bias = lax.dynamic_index_in_dim(outer[10:], me, 0, keepdims=False)
        *normed_two, near = gather_rows(
            (normal_two * params[6] + params[7]).astype(BF),
            lambda values: hidden_forward(values, hidden_pack, inner_bias),
        )
        far = hidden_forward(normed_two[1], hidden_pack, inner_bias)
        second_branch = scatter_rows(near[2], far[2])[0] + params[8]
        saved.append(
            (
                normal,
                inverse,
                normed_all,
                triple,
                log_total,
                mixed,
                branch,
                normal_two,
                inverse_two,
                normed_two,
                (near[0], far[0]),
                (near[1], far[1]),
                second_branch,
            )
        )
        hidden = middle + params[9] * second_branch

    own_position = me * rows + jnp.arange(rows, dtype=jnp.int32)
    grad_hidden = (
        to_inner(cotangent).astype(F32) * (own_position < live_count).astype(F32)[:, None]
    )
    vector_grads = [None] * LAYERS
    norm_grads = [None] * LAYERS
    for layer in range(LAYERS - 1, -1, -1):
        attend_full, output_full, hidden_pack = packs[layer]
        params = vectors[layer * vector_rows : (layer + 1) * vector_rows]
        (
            normal,
            inverse,
            normed_all,
            triple,
            log_total,
            mixed,
            branch,
            normal_two,
            inverse_two,
            normed_two,
            active,
            slope,
            second_branch,
        ) = saved[layer]
        reduce_rows = (params[9] * grad_hidden).astype(BF)
        scale_two_grad = jnp.sum(grad_hidden * second_branch, axis=0)
        shift_out_grad = jnp.sum(reduce_rows.astype(F32), axis=0)
        *reduce_all, near = gather_rows(
            reduce_rows, lambda values: hidden_backward(values, slope[0], hidden_pack)
        )
        far = hidden_backward(reduce_all[1], slope[1], hidden_pack)
        inner_bias_grad = near[1] + far[1]
        hidden_sums = [
            [(normed_two[0], near[0]), (normed_two[1], far[0])],
            [(reduce_all[0], active[0]), (reduce_all[1], active[1])],
        ]
        if layer == LAYERS - 1:
            pack = weight_grads(hidden_sums, F32)
            normed_two_grad, pack = scatter_rows(near[2], far[2], pack)
            early = sum_pack(pack)
        else:
            pack = weight_grads(attend_sums + hidden_sums, BF)
            normed_two_grad, (pack, early) = scatter_rows(near[2], far[2], (pack, early))
            later = sum_pack(pack)
        middle_extra, gain_two_grad, shift_two_grad = norm_back(
            normal_two, inverse_two, params[6], normed_two_grad
        )
        grad_middle = grad_hidden + middle_extra
        branch_rows = (params[5] * grad_middle).astype(BF)
        scale_one_grad = jnp.sum(grad_middle * branch, axis=0)
        shift_att_grad = jnp.sum(branch_rows.astype(F32), axis=0)
        branch_all = jnp.concatenate(gather_rows(branch_rows)[:2], axis=0)
        mixed_grad = dot(branch_all, output_full).astype(BF)
        triple_grad = attention_backward(triple, log_total, mixed_grad, allowed)
        triple_sums = jnp.sum(triple_grad.astype(F32), axis=0).reshape(3, width)
        attend_sums = [[(normed_all, triple_grad)], [(branch_all, mixed)]]
        outer_rows = to_inner(
            jnp.stack(
                [place(triple_sums[0], me), place(triple_sums[2], me), inner_bias_grad[0]]
            )
        )
        vector_grads[layer] = [
            outer_rows[0],
            outer_rows[1],
            shift_att_grad,
            scale_one_grad,
            gain_two_grad,
            shift_two_grad,
            shift_out_grad,
            scale_two_grad,
            outer_rows[2],
        ]
        normed_part = dot_t(triple_grad, attend_full)
        if layer == 0:
            norm_grads[0] = (
                jnp.sum(normed_part * first_normal, axis=0),
                jnp.sum(normed_part, axis=0),
            )
            last = weight_grads(
                attend_sums,
                BF,
                vector_grads[0] + vector_grads[1] + list(norm_grads[0]) + list(norm_grads[1]),
            )
            last, normed_part, early = lax.optimization_barrier(
                (last, normed_part, sum_pair(early, low_row))
            )
            last = lax.all_to_all(last, ("z", "x", "yl"), 0, 0, tiled=True)
        normed_grad, _ = scatter_rows(normed_part[: 2 * rows], normed_part[2 * rows :])
        hidden_extra, *norm_rows = norm_back(normal, inverse, params[0], normed_grad)
        if layer > 0:
            norm_grads[layer] = norm_rows
        grad_hidden = grad_middle + hidden_extra


    last = jnp.sum(last.reshape(-1, feats, last.shape[1]).astype(F32), axis=0)
    later = sum_pair(later, low_row)
    kinds = len(vector_grads[0])
    count = LAYERS * kinds + 4
    table = (last[:, cuts[1] : cuts[1] + count] + last[:, cuts[1] + count : cuts[1] + 2 * count]).T
    ours = (jnp.arange(4, dtype=jnp.int32) == me).astype(F32)[:, None]
    vector_sum = jnp.stack(
        [
            jnp.concatenate(
                [
                    norms,
                    table[start : start + kinds - 1],
                    ours * table[start + kinds - 1 : start + kinds],
                ],
                0,
            )
            for start, norms in (
                (0, table[2 * kinds : 2 * kinds + 2]),
                (kinds, table[2 * kinds + 2 : 2 * kinds + 4]),
            )
        ]
    )
    vector_sum = vector_sum + swap(vector_sum, "core")
    vector_sum = vector_sum + swap(vector_sum, "yh")
    attend_sum = jnp.stack([last[:, : cuts[0]], later[:, : cuts[0]]])
    output_sum = jnp.stack([last[:, cuts[0] : cuts[1]], later[:, cuts[0] : cuts[1]]])
    expand_sum = jnp.stack(
        [later[:, cuts[1] : cuts[2]], early[:, :hidden_width]]
    )
    reduce_sum = jnp.stack([later[:, cuts[2] :], early[:, hidden_width:]])
    reduced = (
        attend_sum.reshape(attend_weight.shape),
        jnp.swapaxes(output_sum, 1, 2),
        expand_sum,
        jnp.swapaxes(reduce_sum, 1, 2),
        vector_sum,
    )
    weights = (attend_weight, output_weight, expand_weight, reduce_weight, vector_params)
    firsts = (attend_first, output_first, expand_first, reduce_first, vector_first)
    seconds = (attend_second, output_second, expand_second, reduce_second, vector_second)
    rates = (D ** (-0.5), 4.0 * D ** (-0.5), D ** (-0.5), FF ** (-0.5), 0.25)
    decays = (0.05, 0.05, 0.05, 0.05, 0.0)
    results = [
        adamw(
            weights[member],
            firsts[member],
            seconds[member],
            reduced[member],
            rates[member],
            decays[member],
        )
        for member in range(5)
    ]
    return (to_outer(hidden), to_outer(grad_hidden)) + tuple(
        results[member][kind] for kind in range(3) for member in range(5)
    )


def solution(mesh):
    fine = Mesh(mesh.devices.reshape(4, 2, 4, 2, 2), DP + MP)
    rows = P(DP + MP, None)
    attend = P(None, DP, None, MP)
    output = P(None, MP, DP)
    expand = P(None, DP, MP)
    vector = P(None, None, DP)
    params = (attend, output, expand, output, vector)
    return jax.shard_map(
        per_device,
        mesh=fine,
        in_specs=(rows, rows, P(DP, None), P(DP)) + params * 3,
        out_specs=(rows, rows) + params * 3,
        check_vma=False,
    )
```

```python
import jax
import jax.numpy as jnp
from jax import lax
from jax.experimental import pallas as pl
from jax.experimental.pallas import tpu as pltpu
from jax.sharding import Mesh, PartitionSpec as P

D = 1024
HD = 64
FF = 4096
LAYERS = 2
STEP = 10
BF = jnp.bfloat16
F32 = jnp.float32
DP = ("z", "yl", "x")
MP = ("yh", "core")


def swap(values, axis):
    return lax.ppermute(values, axis, [(0, 1), (1, 0)])


def to_inner(values):
    lead = values.shape[:-1]
    return jnp.swapaxes(values.reshape(lead + (4, 2, 4, 32)), -3, -2).reshape(lead + (D,))


def to_outer(values):
    lead = values.shape[:-1]
    return jnp.swapaxes(values.reshape(lead + (4, 4, 2, 32)), -3, -2).reshape(lead + (D,))


def gather_rows(values, work=None):
    across = swap(values, "yh")
    near = (values, swap(values, "core"))
    done = None
    if work is not None:
        across, done = lax.optimization_barrier((across, work(near)))
    return near, (across, swap(across, "core")), done


def scatter_rows(near, far, work=None):
    chip = far[0] + swap(far[1], "core")
    other = swap(chip.astype(BF), "yh")
    if work is not None:
        other, work = lax.optimization_barrier((other, work))
    return near[0] + swap(near[1], "core") + other.astype(F32), work


def quarters(values):
    rows = values.shape[0] // 4
    parts = [values[k * rows : (k + 1) * rows] for k in range(4)]
    return parts[:2], parts[2:]


def dot(left, right):
    return jnp.dot(left, right, preferred_element_type=F32)


def dot_t(left, right):
    return jnp.einsum("rf,df->rd", left, right, preferred_element_type=F32)


def dot_first(left, right):
    return lax.dot_general(left, right, (((0,), (0,)), ((), ())), preferred_element_type=F32)


def dot_last(left, right):
    return lax.dot_general(left, right, (((1,), (1,)), ((), ())), preferred_element_type=F32)


def kernel_cost(flops, size, transcendentals=0):
    return pl.CostEstimate(flops=flops, bytes_accessed=size, transcendentals=transcendentals)


def weight_grads(sums, out_type, vectors=()):
    feats = sums[0][0][0][0].shape[1]
    depths = [[sum(part.shape[0] for part in lefts) for lefts, _ in pairs] for pairs in sums]
    last_rows = [
        [right.shape[0] != depth for (_, right), depth in zip(pairs, member)]
        for pairs, member in zip(sums, depths)
    ]
    widths = [
        pairs[0][1].shape[0] if turned[0] else pairs[0][1].shape[1]
        for pairs, turned in zip(sums, last_rows)
    ]
    total = sum(widths) + (128 if vectors else 0)
    count = len(vectors)
    block = 256
    specs, operands = [], []
    for pairs in sums:
        for lefts, right in pairs:
            for left in lefts:
                specs.append(pl.BlockSpec((left.shape[0], block), lambda i: (0, i)))
            specs.append(pl.BlockSpec(right.shape, lambda i: (0, 0)))
            operands += [*lefts, right]
    for values in vectors:
        specs.append(pl.BlockSpec((1, block), lambda i: (0, i)))
        operands.append(values.reshape(1, feats))

    def kernel(*refs):
        refs = list(refs)
        table = refs.pop() if vectors else None
        out_ref = refs.pop()
        start = 0
        for width, pairs, turned in zip(widths, sums, last_rows):
            acc = None
            for (lefts, _), is_turned in zip(pairs, turned):
                left = jnp.concatenate([refs.pop(0)[...] for _ in lefts], axis=0)
                right = refs.pop(0)[...]
                part = lax.dot_general(
                    left,
                    right,
                    (((0,), (1 if is_turned else 0,)), ((), ())),
                    preferred_element_type=F32,
                )
                acc = part if acc is None else acc + part
            out_ref[:, start : start + width] = acc.astype(out_type)
            start += width
        if vectors:
            table[...] = jnp.zeros_like(table)
            for index, row in enumerate(refs):
                values = row[...]
                high = values.astype(BF).astype(F32)
                table[index : index + 1, :] = high
                table[count + index : count + index + 1, :] = values - high
            spots = lax.broadcasted_iota(jnp.int32, (128, 128), 0)
            eye = (spots == lax.broadcasted_iota(jnp.int32, (128, 128), 1)).astype(BF)
            out_ref[:, start:] = dot_first(table[...].astype(BF), eye).astype(out_type)

    depth = sum(depths[0])
    return pl.pallas_call(
        kernel,
        grid=(feats // block,),
        in_specs=specs,
        out_specs=pl.BlockSpec((block, total), lambda i: (i, 0)),
        out_shape=pltpu.HBM((feats, total), out_type),
        scratch_shapes=[pltpu.VMEM((128, block), F32)] if vectors else [],
        compiler_params=pltpu.CompilerParams(vmem_limit_bytes=40 * 2**20),
        cost_estimate=kernel_cost(2 * depth * feats * total, feats * total * 4),
    )(*operands)


def hidden_forward(normed, pack, bias):
    rows, feats = normed[0].shape
    width = bias.shape[0]
    block = 256
    steps = width // block

    def kernel(
        own_ref, mate_ref, expand_ref, reduce_ref, bias_ref, active_ref, slope_ref, *part_refs
    ):
        both = jnp.concatenate([own_ref[...], mate_ref[...]], axis=0)
        inner = dot(both, expand_ref[...]) + bias_ref[...]
        half = 0.5 * (1.0 + lax.erf(inner * 0.5**0.5))
        active = (inner * half).astype(BF)
        active_ref[...] = active
        slope_ref[...] = half + inner * jnp.exp(-0.5 * inner * inner) * (0.5 / jnp.pi) ** 0.5
        part = dot_last(active, reduce_ref[...])

        @pl.when(pl.program_id(0) == 0)
        def _():
            part_refs[0][...] = part[:rows]
            part_refs[1][...] = part[rows:]

        @pl.when(pl.program_id(0) > 0)
        def _():
            part_refs[0][...] += part[:rows]
            part_refs[1][...] += part[rows:]

    chunk = pl.BlockSpec((2 * rows, block), lambda i: (0, i))
    whole = pl.BlockSpec((rows, feats), lambda i: (0, 0))
    return pl.pallas_call(
        kernel,
        grid=(steps,),
        in_specs=[
            whole,
            whole,
            pl.BlockSpec((feats, block), lambda i: (0, i)),
            pl.BlockSpec((feats, block), lambda i: (0, i + steps)),
            pl.BlockSpec((1, block), lambda i: (0, i)),
        ],
        out_specs=[chunk, chunk, whole, whole],
        out_shape=[
            jax.ShapeDtypeStruct((2 * rows, width), BF),
            jax.ShapeDtypeStruct((2 * rows, width), F32),
            jax.ShapeDtypeStruct((rows, feats), F32),
            jax.ShapeDtypeStruct((rows, feats), F32),
        ],
        compiler_params=pltpu.CompilerParams(vmem_limit_bytes=32 * 2**20),
        cost_estimate=kernel_cost(8 * rows * feats * width, 8 * 2**20, 4 * rows * width),
    )(*normed, *[pltpu.with_memory_space_constraint(pack, pltpu.HBM)] * 2, bias.reshape(1, width))


def hidden_backward(grads, slope, pack):
    rows, feats = grads[0].shape
    width = slope.shape[1]
    block = 256
    steps = width // block

    def kernel(
        own_ref, mate_ref, slope_ref, expand_ref, reduce_ref, inner_ref, bias_ref, *part_refs
    ):
        both = jnp.concatenate([own_ref[...], mate_ref[...]], axis=0)
        inner_grad = (dot(both, reduce_ref[...]) * slope_ref[...]).astype(BF)
        inner_ref[...] = inner_grad
        bias_ref[...] = jnp.sum(inner_grad.astype(F32), axis=0, keepdims=True)
        part = dot_last(inner_grad, expand_ref[...])

        @pl.when(pl.program_id(0) == 0)
        def _():
            part_refs[0][...] = part[:rows]
            part_refs[1][...] = part[rows:]

        @pl.when(pl.program_id(0) > 0)
        def _():
            part_refs[0][...] += part[:rows]
            part_refs[1][...] += part[rows:]

    chunk = pl.BlockSpec((2 * rows, block), lambda i: (0, i))
    whole = pl.BlockSpec((rows, feats), lambda i: (0, 0))
    return pl.pallas_call(
        kernel,
        grid=(steps,),
        in_specs=[
            whole,
            whole,
            chunk,
            pl.BlockSpec((feats, block), lambda i: (0, i)),
            pl.BlockSpec((feats, block), lambda i: (0, i + steps)),
        ],
        out_specs=[chunk, pl.BlockSpec((1, block), lambda i: (0, i)), whole, whole],
        out_shape=[
            jax.ShapeDtypeStruct((2 * rows, width), BF),
            jax.ShapeDtypeStruct((1, width), F32),
            jax.ShapeDtypeStruct((rows, feats), F32),
            jax.ShapeDtypeStruct((rows, feats), F32),
        ],
        compiler_params=pltpu.CompilerParams(vmem_limit_bytes=32 * 2**20),
        cost_estimate=kernel_cost(6 * rows * feats * width, 8 * 2**20),
    )(*grads, slope, *[pltpu.with_memory_space_constraint(pack, pltpu.HBM)] * 2)


def norm_parts(values):
    centre = jnp.mean(values, axis=-1, keepdims=True)
    centred = values - centre
    spread = jnp.mean(centred * centred, axis=-1, keepdims=True)
    inverse = lax.rsqrt(spread + 1e-06)
    return centred * inverse, inverse


def norm_back(normal, inverse, gain, grad):
    scaled = grad * gain
    middle = jnp.mean(scaled, axis=-1, keepdims=True)
    slope = jnp.mean(scaled * normal, axis=-1, keepdims=True)
    return (
        (scaled - middle - normal * slope) * inverse,
        jnp.sum(grad * normal, axis=0),
        jnp.sum(grad, axis=0),
    )


def split_heads(triple):
    rows = triple.shape[0]
    parts = triple.reshape(rows, 3, -1, HD)
    return parts[:, 0], parts[:, 1], parts[:, 2]


def attention_forward(triple, allowed):
    query, key, value = split_heads(triple)
    scores = jnp.einsum("qhd,khd->hqk", query, key, preferred_element_type=F32) * HD ** (-0.5)
    scores = jnp.where(allowed[None], scores, -1e30)
    top_score = jnp.max(scores, axis=-1, keepdims=True)
    weights = jnp.exp(scores - top_score)
    total = jnp.sum(weights, axis=-1, keepdims=True)
    probs = (weights / total).astype(BF)
    mixed = jnp.einsum("hqk,khd->qhd", probs, value, preferred_element_type=F32)
    return mixed.astype(BF).reshape(triple.shape[0], -1), top_score + jnp.log(total)


def attention_backward(triple, log_total, mixed_grad, allowed):
    rows = triple.shape[0]
    query, key, value = split_heads(triple)
    grads = mixed_grad.reshape(rows, -1, HD)
    scale = HD ** (-0.5)
    scores = jnp.einsum("qhd,khd->hqk", query, key, preferred_element_type=F32) * scale
    scores = jnp.where(allowed[None], scores, -1e30)
    probs = jnp.exp(scores - log_total)
    prob_grad = jnp.einsum("qhd,khd->hqk", grads, value, preferred_element_type=F32)
    centre = jnp.sum(probs * prob_grad, axis=-1, keepdims=True)
    score_grad = (probs * (prob_grad - centre)).astype(BF)
    query_grad = jnp.einsum("hqk,khd->qhd", score_grad, key, preferred_element_type=F32) * scale
    key_grad = jnp.einsum("hqk,qhd->khd", score_grad, query, preferred_element_type=F32) * scale
    value_grad = jnp.einsum("hqk,qhd->khd", probs.astype(BF), grads, preferred_element_type=F32)
    stacked = jnp.stack([query_grad, key_grad, value_grad], axis=1)
    return stacked.reshape(rows, -1).astype(BF)


def place(values, me):
    return lax.dynamic_update_slice_in_dim(
        jnp.zeros((D,), F32), values, me * values.shape[0], 0
    )


def adamw(weight, first, second, grad, rate, decay):
    first_new = 0.9 * first + 0.1 * grad
    second_new = 0.999 * second + 0.001 * grad * grad
    scaled = first_new / (1.0 - 0.9**STEP) / (jnp.sqrt(second_new / (1.0 - 0.999**STEP)) + 1e-08)
    return (weight - rate * (scaled + decay * weight), first_new, second_new)


def swap_pair(pack, low_row):
    other = swap(pack, "yl")
    return jnp.where(
        low_row == 0, jnp.concatenate([pack, other], 0), jnp.concatenate([other, pack], 0)
    )


def gather_pair(pair):
    return lax.all_gather(pair, ("z", "x"), axis=0, tiled=True)


def sum_pack(pack):
    return lax.psum_scatter(pack, ("z", "x"), scatter_dimension=0, tiled=True)


def sum_pair(pair, low_row):
    rows = pair.shape[0] // 2
    own = lax.dynamic_slice_in_dim(pair, low_row * rows, rows, 0)
    other = lax.dynamic_slice_in_dim(pair, (1 - low_row) * rows, rows, 0)
    return own.astype(F32) + swap(other, "yl").astype(F32)


def place(values, me):
    return lax.dynamic_update_slice_in_dim(
        jnp.zeros((D,), F32), values, me * values.shape[0], 0
    )


def adamw(weight, first, second, grad, rate, decay):
    first_new = 0.9 * first + 0.1 * grad
    second_new = 0.999 * second + 0.001 * grad * grad
    scaled = first_new / (1.0 - 0.9**STEP) / (jnp.sqrt(second_new / (1.0 - 0.999**STEP)) + 1e-08)
    return (weight - rate * (scaled + decay * weight), first_new, second_new)


def swap_pair(pack, low_row):
    other = swap(pack, "yl")
    return jnp.where(
        low_row == 0, jnp.concatenate([pack, other], 0), jnp.concatenate([other, pack], 0)
    )


def gather_pair(pair):
    return lax.all_gather(pair, ("z", "x"), axis=0, tiled=True)


def scatter_pack(pack, low_row):
    pair = lax.psum_scatter(pack, ("z", "x"), scatter_dimension=0, tiled=True)
    rows = pair.shape[0] // 2
    own = lax.dynamic_slice_in_dim(pair, low_row * rows, rows, 0)
    other = lax.dynamic_slice_in_dim(pair, (1 - low_row) * rows, rows, 0)
    return own.astype(F32) + swap(other, "yl").astype(F32)


def per_device(
    tokens,
    cotangent,
    image_ids,
    valid_counts,
    attend_weight,
    output_weight,
    expand_weight,
    reduce_weight,
    vector_params,
    attend_first,
    output_first,
    expand_first,
    reduce_first,
    vector_first,
    attend_second,
    output_second,
    expand_second,
    reduce_second,
    vector_second,
):
    me = lax.axis_index(MP)
    low_row = lax.axis_index("yl")
    rows = tokens.shape[0]
    width = attend_weight.shape[-1]
    hidden_width = expand_weight.shape[-1]
    feats = attend_weight.shape[1]
    live_count = valid_counts[0]

    attend_low = attend_weight.astype(BF).reshape(LAYERS, feats, 3 * width)
    output_low = jnp.swapaxes(output_weight.astype(BF), 1, 2)
    expand_low = expand_weight.astype(BF)
    reduce_low = jnp.swapaxes(reduce_weight.astype(BF), 1, 2)
    vector_rows = vector_params.shape[1]
    vector_low = vector_params.astype(BF).reshape(LAYERS * vector_rows, feats).T
    vector_low = jnp.pad(vector_low, ((0, 0), (0, 128 - LAYERS * vector_rows)))
    second_pair = swap_pair(
        jnp.concatenate([expand_low[0], reduce_low[0], attend_low[1], output_low[1]], 1), low_row
    )
    second_pack = gather_pair(second_pair)
    first_part = jnp.concatenate([attend_low[0], output_low[0], vector_low], 1)
    first_pack = lax.all_to_all(
        jnp.broadcast_to(first_part[None], (32,) + first_part.shape).reshape(
            -1, first_part.shape[1]
        ),
        ("z", "x", "yl"),
        0,
        0,
        tiled=True,
    )
    third_pair = swap_pair(jnp.concatenate([expand_low[1], reduce_low[1]], 1), low_row)
    tokens_in = to_inner(tokens)
    tokens_near, tokens_far, _ = gather_rows(tokens_in)
    tokens_all = jnp.concatenate(tokens_near + tokens_far, axis=0)
    tokens_all, third_pair = lax.optimization_barrier((tokens_all, third_pair))
    third_pack = gather_pair(third_pair)
    cuts = (3 * width, 4 * width, 4 * width + hidden_width, 4 * width + 2 * hidden_width)
    packs = (
        (first_pack[:, : cuts[0]], first_pack[:, cuts[0] : cuts[1]], second_pack),
        (
            second_pack[:, 2 * hidden_width : 2 * hidden_width + cuts[0]],
            second_pack[:, 2 * hidden_width + cuts[0] :],
            third_pack,
        ),
    )
    vectors = lax.dot_general(
        jnp.eye(LAYERS * vector_rows, 128, dtype=BF),
        first_pack[:, cuts[1] :],
        (((1,), (1,)), ((), ())),
        preferred_element_type=F32,
    )
    vectors_outer = to_outer(vectors)

    image_parts = image_ids[0].reshape(4, rows)
    image_row = jnp.concatenate([image_parts[me ^ k] for k in range(4)])
    position = jnp.concatenate(
        [(me ^ k) * rows + jnp.arange(rows, dtype=jnp.int32) for k in range(4)]
    )
    allowed = (image_row[:, None] == image_row[None, :]) & (
        (position[None, :] < live_count) | (position[:, None] == position[None, :])
    )

    first_normal, first_inverse = norm_parts(tokens_all.astype(F32))
    hidden = tokens_in.astype(F32)
    saved = []
    for layer in range(LAYERS):
        attend_full, output_full, hidden_pack = packs[layer]
        params = vectors[layer * vector_rows : (layer + 1) * vector_rows]
        outer = vectors_outer[layer * vector_rows : (layer + 1) * vector_rows]
        if layer == 0:
            normed_all = (first_normal * params[0] + params[1]).astype(BF)
            normed_parts = (normed_all,)
            normal, inverse = first_normal[:rows], first_inverse[:rows]
        else:
            normal, inverse = norm_parts(hidden)
            near, far, _ = gather_rows((normal * params[0] + params[1]).astype(BF))
            normed_parts = near + far
            normed_all = jnp.concatenate(normed_parts, axis=0)
        bias = jnp.concatenate(
            [
                lax.dynamic_slice_in_dim(outer[2], me * width, width, 0),
                jnp.zeros((width,), F32),
                lax.dynamic_slice_in_dim(outer[3], me * width, width, 0),
            ]
        )
        triple = (dot(normed_all, attend_full) + bias).astype(BF)
        mixed, log_total = attention_forward(triple, allowed)
        branch = scatter_rows(*quarters(dot_t(mixed, output_full)))[0] + params[4]
        middle = hidden + params[5] * branch
        normal_two, inverse_two = norm_parts(middle)
        inner_bias = lax.dynamic_index_in_dim(outer[10:], me, 0, keepdims=False)
        *normed_two, near = gather_rows(
            (normal_two * params[6] + params[7]).astype(BF),
            lambda values: hidden_forward(values, hidden_pack, inner_bias),
        )
        far = hidden_forward(normed_two[1], hidden_pack, inner_bias)
        parts = (near[2:], far[2:])
        second_branch = scatter_rows(*parts)[0] + params[8] if layer < LAYERS - 1 else None
        saved.append(
            (
                normal,
                inverse,
                normed_parts,
                triple,
                log_total,
                mixed,
                branch,
                normal_two,
                inverse_two,
                normed_two,
                (near[0], far[0]),
                (near[1], far[1]),
                second_branch,
            )
        )
        if layer < LAYERS - 1:
            hidden = middle + params[9] * second_branch

    own_position = me * rows + jnp.arange(rows, dtype=jnp.int32)
    grad_hidden = (
        to_inner(cotangent).astype(F32) * (own_position < live_count).astype(F32)[:, None]
    )
    vector_grads = [None] * LAYERS
    norm_grads = [None] * LAYERS
    for layer in range(LAYERS - 1, -1, -1):
        attend_full, output_full, hidden_pack = packs[layer]
        params = vectors[layer * vector_rows : (layer + 1) * vector_rows]
        (
            normal,
            inverse,
            normed_parts,
            triple,
            log_total,
            mixed,
            branch,
            normal_two,
            inverse_two,
            normed_two,
            active,
            slope,
            second_branch,
        ) = saved[layer]
        reduce_rows = (params[9] * grad_hidden).astype(BF)
        outer_grad = grad_hidden
        shift_out_grad = jnp.sum(reduce_rows.astype(F32), axis=0)
        *reduce_all, near = gather_rows(
            reduce_rows, lambda values: hidden_backward(values, slope[0], hidden_pack)
        )
        far = hidden_backward(reduce_all[1], slope[1], hidden_pack)
        inner_bias_grad = near[1] + far[1]
        hidden_sums = [
            [(normed_two[0], near[0]), (normed_two[1], far[0])],
            [(reduce_all[0], active[0]), (reduce_all[1], active[1])],
        ]
        if layer == LAYERS - 1:
            pack = weight_grads(hidden_sums, BF)
            pack, near, far = lax.optimization_barrier((pack, near[2:], far[2:]))
            early = sum_pack(pack)
            normed_two_grad, _ = scatter_rows(near, far)
        else:
            pack = weight_grads(attend_sums + hidden_sums, BF)
            normed_two_grad, (pack, early) = scatter_rows(near[2:], far[2:], (pack, early))
            later = sum_pack(pack)
        middle_extra, gain_two_grad, shift_two_grad = norm_back(
            normal_two, inverse_two, params[6], normed_two_grad
        )
        grad_middle = grad_hidden + middle_extra
        branch_rows = (params[5] * grad_middle).astype(BF)
        scale_one_grad = jnp.sum(grad_middle * branch, axis=0)
        shift_att_grad = jnp.sum(branch_rows.astype(F32), axis=0)
        near, far, _ = gather_rows(branch_rows)
        branch_parts = near + far
        if layer == LAYERS - 1:
            branch_parts, parts = lax.optimization_barrier((branch_parts, parts))
            second_branch = scatter_rows(*parts)[0] + params[8]
            hidden = middle + params[9] * second_branch
        scale_two_grad = jnp.sum(outer_grad * second_branch, axis=0)
        branch_all = jnp.concatenate(branch_parts, axis=0)
        mixed_grad = dot(branch_all, output_full).astype(BF)
        triple_grad = attention_backward(triple, log_total, mixed_grad, allowed)
        triple_sums = jnp.sum(triple_grad.astype(F32), axis=0).reshape(3, width)
        attend_sums = [[(normed_parts, triple_grad.T)], [(branch_parts, mixed.T)]]
        outer_rows = to_inner(
            jnp.stack(
                [place(triple_sums[0], me), place(triple_sums[2], me), inner_bias_grad[0]]
            )
        )
        vector_grads[layer] = [
            outer_rows[0],
            outer_rows[1],
            shift_att_grad,
            scale_one_grad,
            gain_two_grad,
            shift_two_grad,
            shift_out_grad,
            scale_two_grad,
            outer_rows[2],
        ]
        normed_part = dot_t(triple_grad, attend_full)
        if layer == 0:
            norm_grads[0] = (
                jnp.sum(normed_part * first_normal, axis=0),
                jnp.sum(normed_part, axis=0),
            )
            last = weight_grads(
                attend_sums,
                BF,
                vector_grads[0] + vector_grads[1] + list(norm_grads[0]) + list(norm_grads[1]),
            )
            last, normed_part, early = lax.optimization_barrier(
                (last, normed_part, sum_pair(early, low_row))
            )
            last = lax.all_to_all(last, ("z", "x", "yl"), 0, 0, tiled=True)
        normed_grad, _ = scatter_rows(*quarters(normed_part))
        hidden_extra, *norm_rows = norm_back(normal, inverse, params[0], normed_grad)
        if layer > 0:
            norm_grads[layer] = norm_rows
        grad_hidden = grad_middle + hidden_extra


    last = jnp.sum(last.reshape(-1, feats, last.shape[1]).astype(F32), axis=0)
    later = sum_pair(later, low_row)
    kinds = len(vector_grads[0])
    count = LAYERS * kinds + 4
    table = (last[:, cuts[1] : cuts[1] + count] + last[:, cuts[1] + count : cuts[1] + 2 * count]).T
    ours = (jnp.arange(4, dtype=jnp.int32) == me).astype(F32)[:, None]
    vector_sum = jnp.stack(
        [
            jnp.concatenate(
                [
                    norms,
                    table[start : start + kinds - 1],
                    ours * table[start + kinds - 1 : start + kinds],
                ],
                0,
            )
            for start, norms in (
                (0, table[2 * kinds : 2 * kinds + 2]),
                (kinds, table[2 * kinds + 2 : 2 * kinds + 4]),
            )
        ]
    )
    vector_sum = vector_sum + swap(vector_sum, "core")
    vector_sum = vector_sum + swap(vector_sum, "yh")
    attend_sum = jnp.stack([last[:, : cuts[0]], later[:, : cuts[0]]])
    output_sum = jnp.stack([last[:, cuts[0] : cuts[1]], later[:, cuts[0] : cuts[1]]])
    expand_sum = jnp.stack(
        [later[:, cuts[1] : cuts[2]], early[:, :hidden_width]]
    )
    reduce_sum = jnp.stack([later[:, cuts[2] :], early[:, hidden_width:]])
    reduced = (
        attend_sum.reshape(attend_weight.shape),
        jnp.swapaxes(output_sum, 1, 2),
        expand_sum,
        jnp.swapaxes(reduce_sum, 1, 2),
        vector_sum,
    )
    weights = (attend_weight, output_weight, expand_weight, reduce_weight, vector_params)
    firsts = (attend_first, output_first, expand_first, reduce_first, vector_first)
    seconds = (attend_second, output_second, expand_second, reduce_second, vector_second)
    rates = (D ** (-0.5), 4.0 * D ** (-0.5), D ** (-0.5), FF ** (-0.5), 0.25)
    decays = (0.05, 0.05, 0.05, 0.05, 0.0)
    results = [
        adamw(
            weights[member],
            firsts[member],
            seconds[member],
            reduced[member],
            rates[member],
            decays[member],
        )
        for member in range(5)
    ]
    return (to_outer(hidden), to_outer(grad_hidden)) + tuple(
        results[member][kind] for kind in range(3) for member in range(5)
    )


def solution(mesh):
    fine = Mesh(mesh.devices.reshape(4, 2, 4, 2, 2), DP + MP)
    rows = P(DP + MP, None)
    attend = P(None, DP, None, MP)
    output = P(None, MP, DP)
    expand = P(None, DP, MP)
    vector = P(None, None, DP)
    params = (attend, output, expand, output, vector)
    return jax.shard_map(
        per_device,
        mesh=fine,
        in_specs=(rows, rows, P(DP, None), P(DP)) + params * 3,
        out_specs=(rows, rows) + params * 3,
        check_vma=False,
    )
```

```python
import jax
import jax.numpy as jnp
from jax import lax
from jax.experimental import pallas as pl
from jax.experimental.pallas import tpu as pltpu
from jax.sharding import Mesh, PartitionSpec as P

D = 1024
HD = 64
FF = 4096
LAYERS = 2
STEP = 10
BF = jnp.bfloat16
F32 = jnp.float32
DP = ("z", "yl", "x")
MP = ("yh", "core")


def swap(values, axis):
    return lax.ppermute(values, axis, [(0, 1), (1, 0)])


def to_inner(values):
    lead = values.shape[:-1]
    return jnp.swapaxes(values.reshape(lead + (4, 2, 4, 32)), -3, -2).reshape(lead + (D,))


def to_outer(values):
    lead = values.shape[:-1]
    return jnp.swapaxes(values.reshape(lead + (4, 4, 2, 32)), -3, -2).reshape(lead + (D,))


def gather_rows(values, work=None):
    across = swap(values, "yh")
    near = (values, swap(values, "core"))
    done = None
    if work is not None:
        across, done = lax.optimization_barrier((across, work(near)))
    return near, (across, swap(across, "core")), done


def scatter_rows(near, far, work=None):
    chip = far[0] + swap(far[1], "core")
    other = swap(chip.astype(BF), "yh")
    if work is not None:
        other, work = lax.optimization_barrier((other, work))
    return near[0] + swap(near[1], "core") + other.astype(F32), work


def quarters(values):
    rows = values.shape[0] // 4
    parts = [values[k * rows : (k + 1) * rows] for k in range(4)]
    return parts[:2], parts[2:]


def dot(left, right):
    return jnp.dot(left, right, preferred_element_type=F32)


def dot_t(left, right):
    return jnp.einsum("rf,df->rd", left, right, preferred_element_type=F32)


def dot_first(left, right):
    return lax.dot_general(left, right, (((0,), (0,)), ((), ())), preferred_element_type=F32)


def dot_last(left, right):
    return lax.dot_general(left, right, (((1,), (1,)), ((), ())), preferred_element_type=F32)


def kernel_cost(flops, size, transcendentals=0):
    return pl.CostEstimate(flops=flops, bytes_accessed=size, transcendentals=transcendentals)


def weight_grads(sums, out_type, vectors=()):
    feats = sums[0][0][0][0].shape[1]
    depths = [[sum(part.shape[0] for part in lefts) for lefts, _ in pairs] for pairs in sums]
    last_rows = [
        [right.shape[0] != depth for (_, right), depth in zip(pairs, member)]
        for pairs, member in zip(sums, depths)
    ]
    widths = [
        pairs[0][1].shape[0] if turned[0] else pairs[0][1].shape[1]
        for pairs, turned in zip(sums, last_rows)
    ]
    total = sum(widths) + (128 if vectors else 0)
    count = len(vectors)
    block = 256
    specs, operands = [], []
    for pairs in sums:
        for lefts, right in pairs:
            for left in lefts:
                specs.append(pl.BlockSpec((left.shape[0], block), lambda i: (0, i)))
            specs.append(pl.BlockSpec(right.shape, lambda i: (0, 0)))
            operands += [pltpu.with_memory_space_constraint(left, pltpu.HBM) for left in lefts]
            operands.append(right)
    for values in vectors:
        specs.append(pl.BlockSpec((1, block), lambda i: (0, i)))
        operands.append(values.reshape(1, feats))

    def kernel(*refs):
        refs = list(refs)
        table = refs.pop() if vectors else None
        out_ref = refs.pop()
        start = 0
        for width, pairs, turned in zip(widths, sums, last_rows):
            acc = None
            for (lefts, _), is_turned in zip(pairs, turned):
                left = jnp.concatenate([refs.pop(0)[...] for _ in lefts], axis=0)
                right = refs.pop(0)[...]
                part = lax.dot_general(
                    left,
                    right,
                    (((0,), (1 if is_turned else 0,)), ((), ())),
                    preferred_element_type=F32,
                )
                acc = part if acc is None else acc + part
            out_ref[:, start : start + width] = acc.astype(out_type)
            start += width
        if vectors:
            table[...] = jnp.zeros_like(table)
            for index, row in enumerate(refs):
                values = row[...]
                high = values.astype(BF).astype(F32)
                table[index : index + 1, :] = high
                table[count + index : count + index + 1, :] = values - high
            spots = lax.broadcasted_iota(jnp.int32, (128, 128), 0)
            eye = (spots == lax.broadcasted_iota(jnp.int32, (128, 128), 1)).astype(BF)
            out_ref[:, start:] = dot_first(table[...].astype(BF), eye).astype(out_type)

    depth = sum(depths[0])
    return pl.pallas_call(
        kernel,
        grid=(feats // block,),
        in_specs=specs,
        out_specs=pl.BlockSpec((block, total), lambda i: (i, 0)),
        out_shape=pltpu.HBM((feats, total), out_type),
        scratch_shapes=[pltpu.VMEM((128, block), F32)] if vectors else [],
        compiler_params=pltpu.CompilerParams(vmem_limit_bytes=24 * 2**20),
        cost_estimate=kernel_cost(2 * depth * feats * total, feats * total * 4),
    )(*operands)


def attention_kernel(normed, pack, first, bias, bias_row, mask):
    rows, feats = mask.shape[0], pack.shape[0]
    width = bias.shape[1]
    heads = width // HD
    count = len(normed)

    def kernel(*refs):
        both = [ref[...] for ref in refs[:count]]
        both = jnp.concatenate(both, axis=0) if count > 1 else both[0]
        query_w, key_w, value_w, output_w, bias_ref, mask_ref = refs[count : count + 6]
        triple_ref, mixed_ref, total_ref = refs[count + 6 : count + 9]
        part_refs = refs[count + 9 :]
        biases = (bias_ref[bias_row : bias_row + 1, :], 0.0, bias_ref[bias_row + 1 : bias_row + 2, :])
        parts = [
            (dot(both, weight[...]) + shift).astype(BF)
            for weight, shift in zip((query_w, key_w, value_w), biases)
        ]
        for index in range(3):
            triple_ref[:, index * width : (index + 1) * width] = parts[index]
        query, key, value = parts
        scaled = query * jnp.asarray(HD ** (-0.5), BF)
        mask_here = mask_ref[...]
        for head in range(heads):
            cols = slice(head * HD, (head + 1) * HD)
            scores = dot_last(scaled[:, cols], key[:, cols]) + mask_here
            top_score = jnp.max(scores, axis=-1, keepdims=True)
            weights = jnp.exp(scores - top_score)
            total = jnp.sum(weights, axis=-1, keepdims=True)
            probs = (weights * (1.0 / total)).astype(BF)
            mixed_ref[:, cols] = dot(probs, value[:, cols]).astype(BF)
            total_ref[:, head : head + 1] = top_score + jnp.log(total)
        part = dot_last(mixed_ref[...], output_w[...])
        size = rows // 4
        for index, part_ref in enumerate(part_refs):
            part_ref[...] = part[index * size : (index + 1) * size]

    whole = lambda values: pl.BlockSpec(values.shape, lambda i: (0, 0))
    column = lambda block: pl.BlockSpec((feats, width), lambda i: (0, block))
    shapes = [
        jax.ShapeDtypeStruct((rows, 3 * width), BF),
        jax.ShapeDtypeStruct((rows, width), BF),
        jax.ShapeDtypeStruct((rows, heads), F32),
    ] + [jax.ShapeDtypeStruct((rows // 4, feats), F32)] * 4
    triple, mixed, total, *parts = pl.pallas_call(
        kernel,
        grid=(1,),
        in_specs=[whole(values) for values in normed]
        + [column(first + index) for index in range(4)]
        + [whole(bias), whole(mask)],
        out_specs=[whole(shape) for shape in shapes],
        out_shape=shapes,
        compiler_params=pltpu.CompilerParams(vmem_limit_bytes=28 * 2**20),
        cost_estimate=kernel_cost(
            2 * rows * width * (4 * feats + 2 * rows), 8 * 2**20, heads * rows * rows
        ),
    )(*normed, *[pltpu.with_memory_space_constraint(pack, pltpu.HBM)] * 4, bias, mask)
    return triple, mixed, total.T[:, :, None], (parts[:2], parts[2:])


def hidden_forward(normed, pack, bias):
    rows, feats = normed[0].shape
    width = bias.shape[0]
    block = 256
    steps = width // block

    def kernel(
        own_ref, mate_ref, expand_ref, reduce_ref, bias_ref, active_ref, slope_ref, *part_refs
    ):
        both = jnp.concatenate([own_ref[...], mate_ref[...]], axis=0)
        inner = dot(both, expand_ref[...]) + bias_ref[...]
        half = 0.5 * (1.0 + lax.erf(inner * 0.5**0.5))
        active = (inner * half).astype(BF)
        active_ref[...] = active
        slope_ref[...] = half + inner * jnp.exp(-0.5 * inner * inner) * (0.5 / jnp.pi) ** 0.5
        part = dot_last(active, reduce_ref[...])

        @pl.when(pl.program_id(0) == 0)
        def _():
            part_refs[0][...] = part[:rows]
            part_refs[1][...] = part[rows:]

        @pl.when(pl.program_id(0) > 0)
        def _():
            part_refs[0][...] += part[:rows]
            part_refs[1][...] += part[rows:]

    chunk = pl.BlockSpec((2 * rows, block), lambda i: (0, i))
    whole = pl.BlockSpec((rows, feats), lambda i: (0, 0))
    return pl.pallas_call(
        kernel,
        grid=(steps,),
        in_specs=[
            whole,
            whole,
            pl.BlockSpec((feats, block), lambda i: (0, i)),
            pl.BlockSpec((feats, block), lambda i: (0, i + steps)),
            pl.BlockSpec((1, block), lambda i: (0, i)),
        ],
        out_specs=[chunk, chunk, whole, whole],
        out_shape=[
            jax.ShapeDtypeStruct((2 * rows, width), BF),
            jax.ShapeDtypeStruct((2 * rows, width), F32),
            jax.ShapeDtypeStruct((rows, feats), F32),
            jax.ShapeDtypeStruct((rows, feats), F32),
        ],
        compiler_params=pltpu.CompilerParams(vmem_limit_bytes=16 * 2**20),
        cost_estimate=kernel_cost(8 * rows * feats * width, 8 * 2**20, 4 * rows * width),
    )(*normed, *[pltpu.with_memory_space_constraint(pack, pltpu.HBM)] * 2, bias.reshape(1, width))


def hidden_backward(grads, slope, pack):
    rows, feats = grads[0].shape
    width = slope.shape[1]
    block = 256
    steps = width // block

    def kernel(
        own_ref, mate_ref, slope_ref, expand_ref, reduce_ref, inner_ref, bias_ref, *part_refs
    ):
        both = jnp.concatenate([own_ref[...], mate_ref[...]], axis=0)
        inner_grad = (dot(both, reduce_ref[...]) * slope_ref[...]).astype(BF)
        inner_ref[...] = inner_grad
        bias_ref[...] = jnp.sum(inner_grad.astype(F32), axis=0, keepdims=True)
        part = dot_last(inner_grad, expand_ref[...])

        @pl.when(pl.program_id(0) == 0)
        def _():
            part_refs[0][...] = part[:rows]
            part_refs[1][...] = part[rows:]

        @pl.when(pl.program_id(0) > 0)
        def _():
            part_refs[0][...] += part[:rows]
            part_refs[1][...] += part[rows:]

    chunk = pl.BlockSpec((2 * rows, block), lambda i: (0, i))
    whole = pl.BlockSpec((rows, feats), lambda i: (0, 0))
    return pl.pallas_call(
        kernel,
        grid=(steps,),
        in_specs=[
            whole,
            whole,
            chunk,
            pl.BlockSpec((feats, block), lambda i: (0, i)),
            pl.BlockSpec((feats, block), lambda i: (0, i + steps)),
        ],
        out_specs=[chunk, pl.BlockSpec((1, block), lambda i: (0, i)), whole, whole],
        out_shape=[
            jax.ShapeDtypeStruct((2 * rows, width), BF),
            jax.ShapeDtypeStruct((1, width), F32),
            jax.ShapeDtypeStruct((rows, feats), F32),
            jax.ShapeDtypeStruct((rows, feats), F32),
        ],
        compiler_params=pltpu.CompilerParams(vmem_limit_bytes=16 * 2**20),
        cost_estimate=kernel_cost(6 * rows * feats * width, 8 * 2**20),
    )(*grads, slope, *[pltpu.with_memory_space_constraint(pack, pltpu.HBM)] * 2)


def norm_parts(values):
    centre = jnp.mean(values, axis=-1, keepdims=True)
    centred = values - centre
    spread = jnp.mean(centred * centred, axis=-1, keepdims=True)
    inverse = lax.rsqrt(spread + 1e-06)
    return centred * inverse, inverse


def norm_back(normal, inverse, gain, grad):
    scaled = grad * gain
    middle = jnp.mean(scaled, axis=-1, keepdims=True)
    slope = jnp.mean(scaled * normal, axis=-1, keepdims=True)
    return (
        (scaled - middle - normal * slope) * inverse,
        jnp.sum(grad * normal, axis=0),
        jnp.sum(grad, axis=0),
    )


def split_heads(triple):
    rows = triple.shape[0]
    parts = triple.reshape(rows, 3, -1, HD)
    return parts[:, 0], parts[:, 1], parts[:, 2]


def attention_backward(triple, log_total, mixed_grad, allowed):
    rows = triple.shape[0]
    query, key, value = split_heads(triple)
    grads = mixed_grad.reshape(rows, -1, HD)
    scale = HD ** (-0.5)
    scores = jnp.einsum("qhd,khd->hqk", query, key, preferred_element_type=F32) * scale
    scores = jnp.where(allowed[None], scores, -1e30)
    probs = jnp.exp(scores - log_total)
    prob_grad = jnp.einsum("qhd,khd->hqk", grads, value, preferred_element_type=F32)
    centre = jnp.sum(probs * prob_grad, axis=-1, keepdims=True)
    score_grad = (probs * (prob_grad - centre)).astype(BF)
    query_grad = jnp.einsum("hqk,khd->qhd", score_grad, key, preferred_element_type=F32) * scale
    key_grad = jnp.einsum("hqk,qhd->khd", score_grad, query, preferred_element_type=F32) * scale
    value_grad = jnp.einsum("hqk,qhd->khd", probs.astype(BF), grads, preferred_element_type=F32)
    stacked = jnp.stack([query_grad, key_grad, value_grad], axis=1)
    return stacked.reshape(rows, -1).astype(BF)


def place(values, me):
    return lax.dynamic_update_slice_in_dim(
        jnp.zeros((D,), F32), values, me * values.shape[0], 0
    )


def adamw(weight, first, second, grad, rate, decay):
    first_new = 0.9 * first + 0.1 * grad
    second_new = 0.999 * second + 0.001 * grad * grad
    scaled = first_new / (1.0 - 0.9**STEP) / (jnp.sqrt(second_new / (1.0 - 0.999**STEP)) + 1e-08)
    return (weight - rate * (scaled + decay * weight), first_new, second_new)


def swap_pair(pack, low_row):
    other = swap(pack, "yl")
    return jnp.where(
        low_row == 0, jnp.concatenate([pack, other], 0), jnp.concatenate([other, pack], 0)
    )


def gather_pair(pair):
    return lax.all_gather(pair, ("z", "x"), axis=0, tiled=True)


def sum_pack(pack):
    return lax.psum_scatter(pack, ("z", "x"), scatter_dimension=0, tiled=True)


def sum_pair(pair, low_row):
    rows = pair.shape[0] // 2
    own = lax.dynamic_slice_in_dim(pair, low_row * rows, rows, 0)
    other = lax.dynamic_slice_in_dim(pair, (1 - low_row) * rows, rows, 0)
    return own.astype(F32) + swap(other, "yl").astype(F32)


def place(values, me):
    return lax.dynamic_update_slice_in_dim(
        jnp.zeros((D,), F32), values, me * values.shape[0], 0
    )


def adamw(weight, first, second, grad, rate, decay):
    first_new = 0.9 * first + 0.1 * grad
    second_new = 0.999 * second + 0.001 * grad * grad
    scaled = first_new / (1.0 - 0.9**STEP) / (jnp.sqrt(second_new / (1.0 - 0.999**STEP)) + 1e-08)
    return (weight - rate * (scaled + decay * weight), first_new, second_new)


def swap_pair(pack, low_row):
    other = swap(pack, "yl")
    return jnp.where(
        low_row == 0, jnp.concatenate([pack, other], 0), jnp.concatenate([other, pack], 0)
    )


def gather_pair(pair):
    return lax.all_gather(pair, ("z", "x"), axis=0, tiled=True)


def scatter_pack(pack, low_row):
    pair = lax.psum_scatter(pack, ("z", "x"), scatter_dimension=0, tiled=True)
    rows = pair.shape[0] // 2
    own = lax.dynamic_slice_in_dim(pair, low_row * rows, rows, 0)
    other = lax.dynamic_slice_in_dim(pair, (1 - low_row) * rows, rows, 0)
    return own.astype(F32) + swap(other, "yl").astype(F32)


def per_device(
    tokens,
    cotangent,
    image_ids,
    valid_counts,
    attend_weight,
    output_weight,
    expand_weight,
    reduce_weight,
    vector_params,
    attend_first,
    output_first,
    expand_first,
    reduce_first,
    vector_first,
    attend_second,
    output_second,
    expand_second,
    reduce_second,
    vector_second,
):
    me = lax.axis_index(MP)
    low_row = lax.axis_index("yl")
    rows = tokens.shape[0]
    width = attend_weight.shape[-1]
    hidden_width = expand_weight.shape[-1]
    feats = attend_weight.shape[1]
    live_count = valid_counts[0]

    attend_low = attend_weight.astype(BF).reshape(LAYERS, feats, 3 * width)
    output_low = jnp.swapaxes(output_weight.astype(BF), 1, 2)
    expand_low = expand_weight.astype(BF)
    reduce_low = jnp.swapaxes(reduce_weight.astype(BF), 1, 2)
    vector_rows = vector_params.shape[1]
    vector_low = vector_params.astype(BF).reshape(LAYERS * vector_rows, feats).T
    vector_low = jnp.pad(vector_low, ((0, 0), (0, 128 - LAYERS * vector_rows)))
    second_pair = swap_pair(
        jnp.concatenate([expand_low[0], reduce_low[0], attend_low[1], output_low[1]], 1), low_row
    )
    second_pack = gather_pair(second_pair)
    first_part = jnp.concatenate([attend_low[0], output_low[0], vector_low], 1)
    first_pack = lax.all_to_all(
        jnp.broadcast_to(first_part[None], (32,) + first_part.shape).reshape(
            -1, first_part.shape[1]
        ),
        ("z", "x", "yl"),
        0,
        0,
        tiled=True,
    )
    third_pair = swap_pair(jnp.concatenate([expand_low[1], reduce_low[1]], 1), low_row)
    tokens_in = to_inner(tokens)
    tokens_near, tokens_far, _ = gather_rows(tokens_in)
    tokens_all = jnp.concatenate(tokens_near + tokens_far, axis=0)
    seeds_near, seeds_far, _ = gather_rows(to_inner(cotangent))
    tokens_all, third_pair, seeds = lax.optimization_barrier(
        (tokens_all, third_pair, seeds_near + seeds_far)
    )
    third_pack = gather_pair(third_pair)
    cuts = (3 * width, 4 * width, 4 * width + hidden_width, 4 * width + 2 * hidden_width)
    packs = (
        (first_pack[:, : cuts[0]], first_pack[:, cuts[0] : cuts[1]], second_pack),
        (
            second_pack[:, 2 * hidden_width : 2 * hidden_width + cuts[0]],
            second_pack[:, 2 * hidden_width + cuts[0] :],
            third_pack,
        ),
    )
    attend_packs = ((first_pack, 0), (second_pack, 2 * hidden_width // width))
    vectors = lax.dot_general(
        jnp.eye(LAYERS * vector_rows, 128, dtype=BF),
        first_pack[:, cuts[1] :],
        (((1,), (1,)), ((), ())),
        preferred_element_type=F32,
    )
    spots = jnp.arange(width, dtype=jnp.int32)
    inner_spots = (spots // 32 % 4) * 64 + (spots // 128) * 32 + spots % 32
    order = (spots[:, None] == inner_spots[None, :]).astype(BF)
    local_vectors = dot(
        lax.dynamic_slice_in_dim(vectors, me * width, width, 1).astype(BF), order
    )

    image_parts = image_ids[0].reshape(4, rows)
    image_row = jnp.concatenate([image_parts[me ^ k] for k in range(4)])
    position = jnp.concatenate(
        [(me ^ k) * rows + jnp.arange(rows, dtype=jnp.int32) for k in range(4)]
    )
    allowed = (image_row[:, None] == image_row[None, :]) & (
        (position[None, :] < live_count) | (position[:, None] == position[None, :])
    )
    mask = jnp.where(allowed, 0.0, -1e30)

    first_normal, first_inverse = norm_parts(tokens_all.astype(F32))
    hidden = tokens_in.astype(F32)
    saved = []
    for layer in range(LAYERS):
        attend_full, output_full, hidden_pack = packs[layer]
        params = vectors[layer * vector_rows : (layer + 1) * vector_rows]
        if layer == 0:
            normed_parts = ((first_normal * params[0] + params[1]).astype(BF),)
            normal, inverse = first_normal[:rows], first_inverse[:rows]
        else:
            normal, inverse = norm_parts(hidden)
            near, far, _ = gather_rows((normal * params[0] + params[1]).astype(BF))
            normed_parts = near + far
        triple, mixed, log_total, branch_halves = attention_kernel(
            normed_parts,
            attend_packs[layer][0],
            attend_packs[layer][1],
            local_vectors,
            layer * vector_rows + 2,
            mask,
        )
        if layer == 0:
            vectors, branch_halves = lax.optimization_barrier((vectors, branch_halves))
        branch = scatter_rows(*branch_halves)[0] + params[4]
        middle = hidden + params[5] * branch
        normal_two, inverse_two = norm_parts(middle)
        inner_bias = to_outer(
            lax.dynamic_index_in_dim(vectors, layer * vector_rows + 10 + me, 0, keepdims=False)
        )
        *normed_two, near = gather_rows(
            (normal_two * params[6] + params[7]).astype(BF),
            lambda values: hidden_forward(values, hidden_pack, inner_bias),
        )
        far = hidden_forward(normed_two[1], hidden_pack, inner_bias)
        parts = (near[2:], far[2:])
        second_branch = scatter_rows(*parts)[0] + params[8] if layer < LAYERS - 1 else None
        saved.append(
            (
                normal,
                inverse,
                normed_parts,
                triple,
                log_total,
                mixed,
                branch,
                normal_two,
                inverse_two,
                normed_two,
                (near[0], far[0]),
                (near[1], far[1]),
                second_branch,
            )
        )
        if layer < LAYERS - 1:
            hidden = middle + params[9] * second_branch

    live = (position < live_count).astype(F32)[:, None]
    seeds = [
        seed.astype(F32) * live[index * rows : (index + 1) * rows]
        for index, seed in enumerate(seeds)
    ]
    grad_hidden = seeds[0]
    vector_grads = [None] * LAYERS
    norm_grads = [None] * LAYERS
    for layer in range(LAYERS - 1, -1, -1):
        attend_full, output_full, hidden_pack = packs[layer]
        params = vectors[layer * vector_rows : (layer + 1) * vector_rows]
        (
            normal,
            inverse,
            normed_parts,
            triple,
            log_total,
            mixed,
            branch,
            normal_two,
            inverse_two,
            normed_two,
            active,
            slope,
            second_branch,
        ) = saved[layer]
        reduce_rows = (params[9] * grad_hidden).astype(BF)
        outer_grad = grad_hidden
        shift_out_grad = jnp.sum(reduce_rows.astype(F32), axis=0)
        if layer == LAYERS - 1:
            reduce_parts = tuple((params[9] * seed).astype(BF) for seed in seeds)
            reduce_all = (reduce_parts[:2], reduce_parts[2:])
            near = hidden_backward(reduce_all[0], slope[0], hidden_pack)
        else:
            *reduce_all, near = gather_rows(
                reduce_rows, lambda values: hidden_backward(values, slope[0], hidden_pack)
            )
        far = hidden_backward(reduce_all[1], slope[1], hidden_pack)
        inner_bias_grad = near[1] + far[1]
        hidden_sums = [
            [(normed_two[0], near[0]), (normed_two[1], far[0])],
            [(reduce_all[0], active[0]), (reduce_all[1], active[1])],
        ]
        if layer == LAYERS - 1:
            pack = weight_grads(hidden_sums, BF)
            pack, near, far = lax.optimization_barrier((pack, near[2:], far[2:]))
            early = sum_pack(pack)
            normed_two_grad, _ = scatter_rows(near, far)
        else:
            pack = weight_grads(attend_sums + hidden_sums, BF)
            normed_two_grad, (pack, early) = scatter_rows(near[2:], far[2:], (pack, early))
            later = sum_pack(pack)
        middle_extra, gain_two_grad, shift_two_grad = norm_back(
            normal_two, inverse_two, params[6], normed_two_grad
        )
        grad_middle = grad_hidden + middle_extra
        branch_rows = (params[5] * grad_middle).astype(BF)
        scale_one_grad = jnp.sum(grad_middle * branch, axis=0)
        shift_att_grad = jnp.sum(branch_rows.astype(F32), axis=0)
        near, far, _ = gather_rows(branch_rows)
        branch_parts = near + far
        if layer == LAYERS - 1:
            branch_parts, parts = lax.optimization_barrier((branch_parts, parts))
            second_branch = scatter_rows(*parts)[0] + params[8]
            hidden = middle + params[9] * second_branch
        scale_two_grad = jnp.sum(outer_grad * second_branch, axis=0)
        branch_all = jnp.concatenate(branch_parts, axis=0)
        mixed_grad = dot(branch_all, output_full).astype(BF)
        triple_grad = attention_backward(triple, log_total, mixed_grad, allowed)
        triple_sums = jnp.sum(triple_grad.astype(F32), axis=0).reshape(3, width)
        attend_sums = [[(normed_parts, triple_grad.T)], [(branch_parts, mixed.T)]]
        outer_rows = to_inner(
            jnp.stack(
                [place(triple_sums[0], me), place(triple_sums[2], me), inner_bias_grad[0]]
            )
        )
        vector_grads[layer] = [
            outer_rows[0],
            outer_rows[1],
            shift_att_grad,
            scale_one_grad,
            gain_two_grad,
            shift_two_grad,
            shift_out_grad,
            scale_two_grad,
            outer_rows[2],
        ]
        normed_part = dot_t(triple_grad, attend_full)
        if layer == 0:
            norm_grads[0] = (
                jnp.sum(normed_part * first_normal, axis=0),
                jnp.sum(normed_part, axis=0),
            )
            last = weight_grads(
                attend_sums,
                BF,
                vector_grads[0] + vector_grads[1] + list(norm_grads[0]) + list(norm_grads[1]),
            )
            last, normed_part, early = lax.optimization_barrier(
                (last, normed_part, sum_pair(early, low_row))
            )
            last = lax.all_to_all(last, ("z", "x", "yl"), 0, 0, tiled=True)
        normed_grad, _ = scatter_rows(*quarters(normed_part))
        hidden_extra, *norm_rows = norm_back(normal, inverse, params[0], normed_grad)
        if layer > 0:
            norm_grads[layer] = norm_rows
        grad_hidden = grad_middle + hidden_extra


    last = jnp.sum(last.reshape(-1, feats, last.shape[1]).astype(F32), axis=0)
    later = sum_pair(later, low_row)
    kinds = len(vector_grads[0])
    count = LAYERS * kinds + 4
    table = (last[:, cuts[1] : cuts[1] + count] + last[:, cuts[1] + count : cuts[1] + 2 * count]).T
    ours = (jnp.arange(4, dtype=jnp.int32) == me).astype(F32)[:, None]
    vector_sum = jnp.stack(
        [
            jnp.concatenate(
                [
                    norms,
                    table[start : start + kinds - 1],
                    ours * table[start + kinds - 1 : start + kinds],
                ],
                0,
            )
            for start, norms in (
                (0, table[2 * kinds : 2 * kinds + 2]),
                (kinds, table[2 * kinds + 2 : 2 * kinds + 4]),
            )
        ]
    )
    vector_sum = vector_sum + swap(vector_sum, "core")
    vector_sum = vector_sum + swap(vector_sum, "yh")
    attend_sum = jnp.stack([last[:, : cuts[0]], later[:, : cuts[0]]])
    output_sum = jnp.stack([last[:, cuts[0] : cuts[1]], later[:, cuts[0] : cuts[1]]])
    expand_sum = jnp.stack(
        [later[:, cuts[1] : cuts[2]], early[:, :hidden_width]]
    )
    reduce_sum = jnp.stack([later[:, cuts[2] :], early[:, hidden_width:]])
    reduced = (
        attend_sum.reshape(attend_weight.shape),
        jnp.swapaxes(output_sum, 1, 2),
        expand_sum,
        jnp.swapaxes(reduce_sum, 1, 2),
        vector_sum,
    )
    weights = (attend_weight, output_weight, expand_weight, reduce_weight, vector_params)
    firsts = (attend_first, output_first, expand_first, reduce_first, vector_first)
    seconds = (attend_second, output_second, expand_second, reduce_second, vector_second)
    rates = (D ** (-0.5), 4.0 * D ** (-0.5), D ** (-0.5), FF ** (-0.5), 0.25)
    decays = (0.05, 0.05, 0.05, 0.05, 0.0)
    results = [
        adamw(
            weights[member],
            firsts[member],
            seconds[member],
            reduced[member],
            rates[member],
            decays[member],
        )
        for member in range(5)
    ]
    return (to_outer(hidden), to_outer(grad_hidden)) + tuple(
        results[member][kind] for kind in range(3) for member in range(5)
    )


def solution(mesh):
    fine = Mesh(mesh.devices.reshape(4, 2, 4, 2, 2), DP + MP)
    rows = P(DP + MP, None)
    attend = P(None, DP, None, MP)
    output = P(None, MP, DP)
    expand = P(None, DP, MP)
    vector = P(None, None, DP)
    params = (attend, output, expand, output, vector)
    return jax.shard_map(
        per_device,
        mesh=fine,
        in_specs=(rows, rows, P(DP, None), P(DP)) + params * 3,
        out_specs=(rows, rows) + params * 3,
        check_vma=False,
    )
```
